512 devices in a mesh: comp: 2 (over core), gx: 64 (over z, y), gz: 4 (over x).
Axes of the slice: x: 4, y: 4, z: 16, core: 2. Of those that a mesh axis runs over, the one named last changes fastest.
Arguments:
- fields: float32 [2, 72, 1024, 512], P('comp', None, 'gx', 'gz'), may hold values from -6 to 6
- diffusivity: float32 [2, 1024, 512], P('comp', 'gx', 'gz'), may hold values from 0.02 to 0.24
- wet_mask: int32 [1024, 512], P('gx', 'gz'), may hold values 0 or 1
- column_op: float32 [2, 72, 72], P('comp'), as said below
- export_scale: float32 [2, 16], P('comp'), may hold values from 0.5 to 2
- import_gain: float32 [2, 16], P('comp'), may hold values from 0.3 to 1
- tile_source: int32 [2, 1024, 4, 3], P('comp', 'gx', 'gz'), may hold values from 0 to 47
- tile_count: int32 [2, 1024, 4], P('comp', 'gx', 'gz'), may hold values from 1 to 3
- remap_tiles: bfloat16 [2, 1024, 4, 3, 128, 128], P('comp', 'gx', 'gz'), may hold values from -0.3125 to 0.3125
Outputs:
- new_fields: float32 [2, 72, 1024, 512], P('comp', None, 'gx', 'gz')
The draws below stay inside these ranges and needn't reach their ends.
Inputs may be any that keep to these rules, and one draw needn't show every extreme that they name: A destination tile in grid rows of one device's block reads tile_source in the other component's rows of the block before it along the first grid dimension (values under 16), its own block (16 to 31), or the block after it. `column_op`: each matrix has diagonal entries 0.7.
All inputs are finite; a program needn't handle non-finite values. No bound on the sum of `wet_mask` on one device may be relied on, other than what follows from the above.
Results may differ from the reference program's by a relative error of at most 0.00072.
Values may be sent and summed in bfloat16 or wider, within the bound.
A program may use at most 64 MiB of HBM per device.

```python
import math
import jax
import jax.numpy as jnp
from jax import lax

LEV = 72
TILE = 128
CX = 16
K = 3
MB = 8
FB = 2
NSUB = 4
NF = 16
NXC = 1024
NZT = 4
NZC = 512


def draw_column_op(key, part):
    key = jax.random.fold_in(key, 11)
    spread = jax.random.normal(key, (2, LEV, LEV), jnp.float32)
    eye_mask = jnp.eye(LEV, dtype=jnp.float32)[None]
    return 0.7 * eye_mask + (1.0 - eye_mask) * spread * (0.3 / LEV ** 0.5)


def plant(entries, own_key, low, top_value):
    shape = entries.shape
    index_at = [jax.random.randint(jax.random.fold_in(own_key, axis), (), 0, shape[axis]) for axis in range(len(shape))]
    entries = entries.at[tuple(index_at)].set(low)
    longest = shape.index(max(shape))
    index_at[longest] = (index_at[longest] + 1) % shape[longest]
    return entries.at[tuple(index_at)].set(top_value)


def levels(rng, dims, split, low, top_value):
    def one(axis_at, blocks):
        steps = jax.random.uniform(jax.random.fold_in(jax.random.fold_in(rng, 6), axis_at), (blocks,), jnp.float32, low / len(split), top_value / len(split))
        return jnp.repeat(jnp.exp(steps), dims[axis_at] // blocks).reshape((-1,) + (1,) * (len(dims) - axis_at - 1))

    loudness = one(*split[0])
    for cut in split[1:]:
        loudness = loudness * one(*cut)
    return loudness


def normal_values(stream_key, extent, width, bound, pieces=(), held_as=jnp.bfloat16):
    values = jax.random.normal(stream_key, extent, jnp.float32) * width
    if len(pieces) > 0:
        values = levels(stream_key, extent, pieces, -0.22, 0.18) * values
    return jnp.clip(values, min=-bound, max=bound).astype(held_as)


def setup_inputs(seed: int = 0) -> dict:
    keys = jax.random.split(jax.random.key(seed), 10)
    fields = normal_values(keys[0], (2, LEV, NXC, NZC), 1.0, 6.0, ((0, 2), (2, 64), (3, 4)), jnp.float32)
    diffusivity = jnp.clip(0.02 + 0.22 * jax.random.uniform(keys[1], (2, NXC, NZC), jnp.float32) ** levels(keys[1], (2, NXC, NZC), ((0, 2), (1, 64), (2, 4)), -0.2, 0.2), 0.02, 0.24)
    wet_mask = plant((jax.random.randint(keys[2], (NXC, NZC), 0, 10) < 7).astype(jnp.int32), jax.random.fold_in(keys[2], 1), 0, 1)
    column_op = draw_column_op(jax.random.fold_in(keys[9], 71), 0)
    export_scale = jnp.clip(jnp.exp(math.log(2.0) - 1.3862944 * jax.random.uniform(keys[4], (2, NF), jnp.float32) ** levels(keys[4], (2, NF), ((0, 2),), -0.2, 0.2)), 0.5, 2.0)
    import_gain = jnp.clip(jnp.exp(math.log(1.0) - 1.2039728 * jax.random.uniform(keys[5], (2, NF), jnp.float32) ** levels(keys[5], (2, NF), ((0, 2),), -0.2, 0.2)), 0.3, 1.0)
    tile_source = plant(jax.random.randint(keys[6], (2, NXC, NZT, K), 0, 3 * CX), jax.random.fold_in(keys[6], 1), 0, (3 * CX) - 1).astype(jnp.int32)
    tile_count = plant(jax.random.randint(keys[7], (2, NXC, NZT), 1, K + 1), jax.random.fold_in(keys[7], 1), 1, K).astype(jnp.int32)
    remap_tiles = normal_values(keys[8], (2, NXC, NZT, K, TILE, TILE), (TILE * K) ** -0.5, 0.3125, ((0, 2), (1, 64), (2, 4)))
    return {"fields": fields, "diffusivity": diffusivity, "wet_mask": wet_mask, "column_op": column_op, "export_scale": export_scale, "import_gain": import_gain, "tile_source": tile_source, "tile_count": tile_count, "remap_tiles": remap_tiles}


def remap(source, src, live, tiles):
    flux_count = source.shape[0]
    blocks = source.reshape(flux_count, NXC, NZT, TILE)
    padded = jnp.pad(blocks, ((0, 0), (CX, CX), (0, 0), (0, 0)))
    columns = jnp.arange(NZT)[:, None]

    def one_row(items):
        index, alive, weights = items
        picked = padded[:, index, columns, :]
        picked = picked * alive.astype(jnp.bfloat16)[None, :, :, None]
        return jnp.einsum('fzkt,zkts->fzs', picked.astype(jnp.float32), weights.astype(jnp.float32))

    rows_out = lax.map(one_row, (src, live, tiles))
    return jnp.transpose(rows_out, (1, 0, 2, 3)).reshape(flux_count, NXC, NZC)


def reference(fields, diffusivity, wet_mask, column_op, export_scale, import_gain, tile_source, tile_count, remap_tiles):
    flux_count = MB * FB
    wet_cells = wet_mask.astype(jnp.float32)
    wets = jnp.stack([jnp.ones_like(wet_cells), wet_cells])
    rate = wets * diffusivity
    rows = jnp.arange(NXC).astype(jnp.int32)
    base = (rows // CX) * CX
    src = base[None, :, None, None] + tile_source
    live = jnp.arange(K).astype(jnp.int32)[None, None, None, :] < tile_count[..., None]
    state = fields
    for step in range(NSUB):
        padded = jnp.pad(state, ((0, 0), (0, 0), (1, 1), (1, 1)))
        beside_all = padded[:, :, 2:, 1:-1] + padded[:, :, :-2, 1:-1] + padded[:, :, 1:-1, 2:] + padded[:, :, 1:-1, :-2]
        smooth = state + rate[:, None] * (beside_all - 4.0 * state)
        column = jnp.einsum('cab,cbxz->caxz', column_op, smooth, precision=lax.Precision.HIGHEST)
        exported = (jnp.tanh(export_scale[:, :, None, None] * column[:, :flux_count]) * wets[:, None]).astype(jnp.bfloat16)
        imported = jnp.stack([remap(exported[1 - c], src[c], live[c], remap_tiles[c]) for c in range(2)])
        top = column[:, :flux_count] + import_gain[:, :, None, None] * wets[:, None] * imported
        state = jnp.concatenate([top, column[:, flux_count:]], axis=1)
    return state
```

```python
import functools

import jax
import jax.numpy as jnp
from jax import lax
from jax.experimental import pallas as pl
from jax.experimental.pallas import tpu as pltpu
from jax.sharding import PartitionSpec as P

NSUB = 4
MESH = pl.DeviceIdType.MESH
F32 = jnp.float32
BF16 = jnp.bfloat16


def lane_ids(shape):
    return lax.broadcasted_iota(jnp.int32, shape, 1)


def split3(value, pad):
    if pad:
        value = jnp.concatenate([value, jnp.zeros((pad, value.shape[1]), F32)], axis=0)
    high = value.astype(BF16)
    low = (value - high.astype(F32)).astype(BF16)
    return [high, high, low]


def kernel(
    dims,
    fields,
    diff,
    wetm,
    op,
    scale,
    gain,
    source,
    count,
    tiles,
    out,
    pad,
    dpad,
    hz,
    dz,
    ex0,
    ex1,
    ex2,
    ex3,
    es,
    ppre,
    last,
    zpack,
    dzpack,
    w,
    rate,
    weti,
    wet,
    ops,
    acat,
    acat16,
    state_sem,
    misc_sem,
    out_sem,
    hx_send,
    hx_recv,
    hz_send,
    hz_recv,
    dx_send,
    dx_recv,
    dz_send,
    dz_recv,
    ex_send,
    ex_recv,
):
    lev, rows, flux, depth = dims
    exs = (ex0, ex1, ex2, ex3)
    groups = lev // 8
    fgroups = flux // 8
    c, gx, gz = lax.axis_index("comp"), lax.axis_index("gx"), lax.axis_index("gz")
    nx, nz = lax.axis_size("gx"), lax.axis_size("gz")
    prev, nxt, left, right = gx > 0, gx < nx - 1, gz > 0, gz < nz - 1
    at_prev, at_next = (c, gx - 1, gz), (c, gx + 1, gz)
    at_left, at_right = (c, gx, gz - 1), (c, gx, gz + 1)
    over = (1 - c, gx, gz)
    over_prev, over_next = (1 - c, gx - 1, gz), (1 - c, gx + 1, gz)

    state_copies = [
        pltpu.make_async_copy(
            fields.at[0, :, r, :], pad.at[0, r + 1], state_sem.at[r]
        )
        for r in range(rows)
    ]
    misc = [
        pltpu.make_async_copy(diff.at[0], rate, misc_sem.at[0]),
        pltpu.make_async_copy(wetm, weti, misc_sem.at[1]),
        pltpu.make_async_copy(op.at[0], ops, misc_sem.at[2]),
    ]
    tile_copy = pltpu.make_async_copy(tiles.at[0, :, 0], w, misc_sem.at[3])
    for copy in state_copies + misc + [tile_copy]:
        copy.start()

    @pl.when(jnp.logical_not(prev))
    def _():
        pad[:, 0] = jnp.zeros((NSUB, lev, 128), F32)
        dpad[:, 0] = jnp.zeros((NSUB - 1, flux, 128), F32)
        for ref in exs:
            ref[0:rows] = jnp.zeros((rows, flux, 128), BF16)

    @pl.when(jnp.logical_not(nxt))
    def _():
        pad[:, rows + 1] = jnp.zeros((NSUB, lev, 128), F32)
        dpad[:, rows + 1] = jnp.zeros((NSUB - 1, flux, 128), F32)
        for ref in exs:
            ref[2 * rows : 3 * rows] = jnp.zeros((rows, flux, 128), BF16)

    @pl.when(jnp.logical_not(left))
    def _():
        hz[:, 0] = jnp.zeros((NSUB, 16, 128), F32)
        dz[:, 0] = jnp.zeros((NSUB - 1, 8, 128), F32)

    @pl.when(jnp.logical_not(right))
    def _():
        hz[:, 1] = jnp.zeros((NSUB, 16, 128), F32)
        dz[:, 1] = jnp.zeros((NSUB - 1, 8, 128), F32)

    for ref in exs:
        ref[3 * rows] = jnp.zeros((flux, 128), BF16)

    barrier = pltpu.get_barrier_semaphore()
    peers = [
        (None, over),
        (prev, over_prev),
        (prev, at_prev),
        (nxt, over_next),
        (nxt, at_next),
        (left, at_left),
        (right, at_right),
    ]

    def when(flag, body):
        if flag is None:
            body()
        else:
            pl.when(flag)(body)

    for flag, peer in peers:
        when(
            flag,
            lambda peer=peer: pl.semaphore_signal(
                barrier, inc=1, device_id=peer, device_id_type=MESH
            ),
        )
    expected = (
        1
        + 2 * prev.astype(jnp.int32)
        + 2 * nxt.astype(jnp.int32)
        + left.astype(jnp.int32)
        + right.astype(jnp.int32)
    )
    pl.semaphore_wait(barrier, expected)

    sent = []

    def remote(flag, src, dst, ssem, rsem, peer, start=True):
        copy = pltpu.make_async_remote_copy(
            src_ref=src,
            dst_ref=dst,
            send_sem=ssem,
            recv_sem=rsem,
            device_id=peer,
            device_id_type=MESH,
        )
        if start:
            when(flag, copy.start)
            sent.append((flag, copy))
        return copy

    def receive(flag, dst, rsem, peer):
        copy = pltpu.make_async_remote_copy(
            src_ref=dst,
            dst_ref=dst,
            send_sem=rsem,
            recv_sem=rsem,
            device_id=peer,
            device_id_type=MESH,
        )
        when(flag, copy.wait_recv)

    def send_rows(first, last_row, box, t, send, recv):
        remote(prev, first, box.at[t, rows + 1], send.at[t, 1], recv.at[t, 1], at_prev)
        remote(nxt, last_row, box.at[t, 0], send.at[t, 0], recv.at[t, 0], at_next)

    def wait_rows(box, t, recv):
        receive(prev, box.at[t, 0], recv.at[t, 0], at_prev)
        receive(nxt, box.at[t, rows + 1], recv.at[t, 1], at_next)

    def send_columns(pack, box, t, send, recv):
        remote(left, pack.at[t, 1], box.at[t, 1], send.at[t, 1], recv.at[t, 1], at_left)
        remote(right, pack.at[t, 0], box.at[t, 0], send.at[t, 0], recv.at[t, 0], at_right)

    def wait_columns(box, t, recv):
        receive(left, box.at[t, 0], recv.at[t, 0], at_left)
        receive(right, box.at[t, 1], recv.at[t, 1], at_right)

    lane8 = lane_ids((8, 128))

    def pack_edges(load, n_groups):
        parts = [[None, None], [None, None]]
        for r in range(rows):
            for g in range(n_groups):
                value = load(r, g)
                half, lane = divmod(g * rows + r, 128)
                for side, have in ((0, 127), (1, 0)):
                    moved = pltpu.roll(value, (lane - have) % 128, 1) if lane != have else value
                    old = parts[side][half]
                    parts[side][half] = (
                        moved if old is None else jnp.where(lane8 == lane, moved, old)
                    )
        return parts

    def stencil(load, packed, n_groups, r):
        here = load(r + 1)
        levels = 8 * n_groups
        lane = lane_ids((levels, 128))
        lefts, rights = [], []
        for g in range(n_groups):
            half, at = divmod(g * rows + r, 128)
            lefts.append(pltpu.roll(packed[0][half], (0 - at) % 128, 1) if at != 0 else packed[0][half])
            rights.append(
                pltpu.roll(packed[1][half], (127 - at) % 128, 1) if at != 127 else packed[1][half]
            )
        before = jnp.where(lane == 0, jnp.concatenate(lefts, axis=0), pltpu.roll(here, 1, 1))
        after = jnp.where(lane == 127, jnp.concatenate(rights, axis=0), pltpu.roll(here, 127, 1))
        beside = load(r + 2) + load(r) + after + before
        return here + rate[r : r + 1, :] * (beside - 4.0 * here)

    send_rows(fields.at[0, :, 0, :], fields.at[0, :, rows - 1, :], pad, 0, hx_send, hx_recv)

    for copy in misc:
        copy.wait()
    ocean = c == 1
    wet[...] = jnp.where(ocean, weti[...].astype(F32), 1.0)
    rate[...] = rate[...] * wet[...]
    matrix = jnp.concatenate([ops[...], jnp.zeros((lev, 128 - lev), F32)], axis=1)
    high = matrix.astype(BF16).astype(F32)
    low = matrix - high
    lane = lane_ids((lev, 128))
    low80 = pltpu.roll(low, 80, 1)
    acat[...] = jnp.concatenate(
        [jnp.where(lane < 80, high, low80), jnp.where(lane < 32, low80, pltpu.roll(high, 32, 1))],
        axis=1,
    ).astype(BF16)
    acat16[...] = jnp.where(
        lane < flux,
        high,
        jnp.where(
            lane < 2 * flux,
            pltpu.roll(low, flux, 1),
            jnp.where(lane < 3 * flux, pltpu.roll(high, 2 * flux, 1), 0.0),
        ),
    ).astype(BF16)
    level = lax.broadcasted_iota(jnp.int32, (flux, 128), 0)
    scales = jnp.zeros((flux, 128), F32)
    gains = jnp.zeros((flux, 128), F32)
    for f in range(flux):
        scales = jnp.where(level == f, scale[0, f], scales)
        gains = jnp.where(level == f, gain[0, f], gains)

    for copy in state_copies:
        copy.wait()

    def group_of(box, t):
        return lambda r, g: box[t, r + 1, 8 * g : 8 * g + 8, :]

    parts = pack_edges(group_of(pad, 0), groups)
    for side in range(2):
        zpack[0, side] = jnp.concatenate(parts[side], axis=0)
    send_columns(zpack, hz, 0, hz_send, hz_recv)

    def column_of(t):
        wait_rows(pad, t, hx_recv)
        wait_columns(hz, t, hz_recv)
        packed = [[hz[t, side, 0:8], hz[t, side, 8:16]] for side in range(2)]
        for p in range(rows // 2):
            halves = []
            for r in (2 * p, 2 * p + 1):
                smooth = stencil(lambda i: pad[t, i], packed, groups, r)
                halves.append(
                    jnp.concatenate(split3(smooth, 80 - lev) + [jnp.zeros((16, 128), BF16)], axis=0)
                )
            both = jnp.dot(
                acat[...], jnp.concatenate(halves, axis=1), preferred_element_type=F32
            )
            ppre[2 * p] = both[:, :128]
            ppre[2 * p + 1] = both[:, 128:]

    column_of(0)
    for t in range(NSUB):
        final = t == NSUB - 1

        def keep(r, value):
            if final:
                last[r] = value
            else:
                pad[t + 1, r + 1] = value

        if t > 0:
            wait_rows(dpad, t - 1, dx_recv)
            wait_columns(dz, t - 1, dz_recv)
            dpacked = [[dz[t - 1, side]] for side in range(2)]
        for p in range(rows // 2):
            pair = [ppre[2 * p], ppre[2 * p + 1]]
            if t > 0:
                halves = []
                for r in (2 * p, 2 * p + 1):
                    smooth = stencil(lambda i: dpad[t - 1, i], dpacked, fgroups, r)
                    halves.append(jnp.concatenate(split3(smooth, 0), axis=0))
                both = jnp.dot(
                    acat16[:, : 3 * flux],
                    jnp.concatenate(halves, axis=1),
                    preferred_element_type=F32,
                )
                pair = [pair[0] + both[:, :128], pair[1] + both[:, 128:]]
            for i, r in enumerate((2 * p, 2 * p + 1)):
                es[t, r] = (jnp.tanh(scales * pair[i][:flux]) * wet[r : r + 1, :]).astype(BF16)
                keep(r, pair[i])
        mine = es.at[t]
        box = exs[t]
        remote(nxt, mine, box.at[0:rows], ex_send.at[t, 0], ex_recv.at[t, 0], over_next)
        remote(prev, mine, box.at[2 * rows : 3 * rows], ex_send.at[t, 2], ex_recv.at[t, 2], over_prev)
        remote(None, mine, box.at[rows : 2 * rows], ex_send.at[t, 1], ex_recv.at[t, 1], over)

        if final:
            rest = [
                pltpu.make_async_copy(
                    last.at[r, flux:], out.at[0, flux:, r, :], out_sem.at[0, r]
                )
                for r in range(rows)
            ]
            for copy in rest:
                copy.start()
        else:
            send_rows(pad.at[t + 1, 1], pad.at[t + 1, rows], pad, t + 1, hx_send, hx_recv)
            parts = pack_edges(group_of(pad, t + 1), groups)
            for side in range(2):
                zpack[t + 1, side] = jnp.concatenate(parts[side], axis=0)
            send_columns(zpack, hz, t + 1, hz_send, hz_recv)

        if t == 0:
            tile_copy.wait()
        receive(prev, box.at[0:rows], ex_recv.at[t, 0], over_prev)
        receive(None, box.at[rows : 2 * rows], ex_recv.at[t, 1], over)
        receive(nxt, box.at[2 * rows : 3 * rows], ex_recv.at[t, 2], over_next)
        for p in range(rows // 2):
            picked, weights = [], []
            for r in (2 * p, 2 * p + 1):
                chosen = []
                for k in range(depth):
                    index = jnp.where(k < count[0, 0, r], source[0, k, 0, r], 3 * rows)
                    chosen.append(box[index])
                picked.append(jnp.concatenate(chosen, axis=1))
                weights.append(w[r].reshape(depth * 128, 128))
            both = jnp.dot(
                jnp.concatenate(picked, axis=0),
                jnp.concatenate(weights, axis=1),
                preferred_element_type=F32,
            )
            for i, r in enumerate((2 * p, 2 * p + 1)):
                value = gains * wet[r : r + 1, :] * both[i * flux : (i + 1) * flux, i * 128 : (i + 1) * 128]
                if final:
                    last[r, 0:flux] += value
                else:
                    dpad[t, r + 1] = value
        if final:
            top = [
                pltpu.make_async_copy(
                    last.at[r, 0:flux], out.at[0, 0:flux, r, :], out_sem.at[1, r]
                )
                for r in range(rows)
            ]
            for copy in top:
                copy.start()
        else:
            send_rows(dpad.at[t, 1], dpad.at[t, rows], dpad, t, dx_send, dx_recv)
            parts = pack_edges(group_of(dpad, t), fgroups)
            for side in range(2):
                dzpack[t, side] = parts[side][0]
            send_columns(dzpack, dz, t, dz_send, dz_recv)
            column_of(t + 1)

    for flag, copy in sent:
        when(flag, copy.wait_send)
    for copy in rest + top:
        copy.wait()


def on_device(*args):
    fields, export_scale, tile_source = args[0], args[4], args[6]
    _, lev, rows, width = fields.shape
    flux, depth = export_scale.shape[1], tile_source.shape[3]
    dma = pltpu.SemaphoreType.DMA
    any_ = pl.BlockSpec(memory_space=pl.ANY)
    smem = pl.BlockSpec(memory_space=pltpu.SMEM)
    vmem = pltpu.VMEM
    box = vmem((3 * rows + 1, flux, width), BF16)
    return pl.pallas_call(
        functools.partial(kernel, (lev, rows, flux, depth)),
        out_shape=jax.ShapeDtypeStruct(fields.shape, F32),
        in_specs=[any_, any_, any_, any_, smem, smem, smem, smem, any_],
        out_specs=any_,
        scratch_shapes=[
            vmem((NSUB, rows + 2, lev, width), F32),
            vmem((NSUB - 1, rows + 2, flux, width), F32),
            vmem((NSUB, 2, 16, width), F32),
            vmem((NSUB - 1, 2, 8, width), F32),
            box,
            box,
            box,
            box,
            vmem((NSUB, rows, flux, width), BF16),
            vmem((rows, lev, width), F32),
            vmem((rows, lev, width), F32),
            vmem((NSUB, 2, 16, width), F32),
            vmem((NSUB - 1, 2, 8, width), F32),
            vmem((rows, depth, width, width), BF16),
            vmem((rows, width), F32),
            vmem((rows, width), jnp.int32),
            vmem((rows, width), F32),
            vmem((lev, lev), F32),
            vmem((lev, 256), BF16),
            vmem((lev, 128), BF16),
            dma((rows,)),
            dma((4,)),
            dma((2, rows)),
            dma((NSUB, 2)),
            dma((NSUB, 2)),
            dma((NSUB, 2)),
            dma((NSUB, 2)),
            dma((NSUB - 1, 2)),
            dma((NSUB - 1, 2)),
            dma((NSUB - 1, 2)),
            dma((NSUB - 1, 2)),
            dma((NSUB, 3)),
            dma((NSUB, 3)),
        ],
        compiler_params=pltpu.CompilerParams(
            collective_id=0, has_side_effects=True, vmem_limit_bytes=56 * 1024 * 1024
        ),
        name="coupled",
    )(*args[:6], jnp.transpose(args[6], (0, 3, 2, 1)), jnp.transpose(args[7], (0, 2, 1)), args[8])


def solution(mesh):
    in_specs = (
        P("comp", None, "gx", "gz"),
        P("comp", "gx", "gz"),
        P("gx", "gz"),
        P("comp", None, None),
        P("comp", None),
        P("comp", None),
        P("comp", "gx", "gz", None),
        P("comp", "gx", "gz"),
        P("comp", "gx", "gz", None, None, None),
    )
    out_specs = P("comp", None, "gx", "gz")
    return jax.shard_map(
        on_device, mesh=mesh, in_specs=in_specs, out_specs=out_specs, check_vma=False
    )
```

```python
import functools

import jax
import jax.numpy as jnp
from jax import lax
from jax.experimental import pallas as pl
from jax.experimental.pallas import tpu as pltpu
from jax.sharding import PartitionSpec as P

NSUB = 4
MESH = pl.DeviceIdType.MESH
F32 = jnp.float32
BF16 = jnp.bfloat16


def lane_ids(shape):
    return lax.broadcasted_iota(jnp.int32, shape, 1)


def split3(value, pad):
    if pad:
        value = jnp.concatenate([value, jnp.zeros((pad, value.shape[1]), F32)], axis=0)
    high = value.astype(BF16)
    low = (value - high.astype(F32)).astype(BF16)
    return [high, high, low]


def place(group, row):
    return group // 4, 32 * (group % 4) + 2 * row


def kernel(dims, fields, diff, wetm, op, scale, gain, source, count, tiles, out, *scratch):
    lev, rows, flux, depth = dims
    (pad, dpad, hz, cp, rp, ppre, last, zpack, cpack, rpack, dsplit, w, wedge, wside, wcol, wcols, wd) = scratch[:17]
    (rate, weti, wet, wetn, wets, gw, ops, acat, acat16) = scratch[17:26]
    exs, ess = scratch[26:30], scratch[30:34]
    eff, eff_same, eff_over = scratch[34:37]
    local_sem, send_sem, recv_sem = scratch[37:40]
    groups, fgroups = lev // 8, flux // 8
    pairs = rows // 2
    c, gx, gz = lax.axis_index("comp"), lax.axis_index("gx"), lax.axis_index("gz")
    nx, nz = lax.axis_size("gx"), lax.axis_size("gz")
    prev, nxt, left, right = gx > 0, gx < nx - 1, gz > 0, gz < nz - 1
    prev2, nxt2 = gx > 1, gx < nx - 2

    def same(dx, dz):
        return (c, gx + dx, gz + dz)

    def over(dx, dz):
        return (1 - c, gx + dx, gz + dz)

    in_x = {-1: prev, 0: None, 1: nxt}

    def both(a, b):
        return b if a is None else a if b is None else jnp.logical_and(a, b)

    def when(flag, todo):
        if flag is None:
            todo()
        else:
            pl.when(flag)(todo)

    local = iter(range(100))

    def fetch(src, dst):
        copy = pltpu.make_async_copy(src, dst, local_sem.at[next(local)])
        copy.start()
        return copy

    state_copies = [fetch(fields.at[0, :, r, :], pad.at[0, r + 1]) for r in range(rows)]
    misc = [fetch(op.at[0], ops), fetch(diff.at[0], rate), fetch(wetm, weti)]
    tile_copy = fetch(tiles.at[0, :, 0], w)

    zeros_w = jnp.zeros((depth, 128, 128), BF16)
    zeros_ex = jnp.zeros((rows, flux, 128), BF16)
    no_source = jnp.concatenate([jnp.zeros((128, 128), BF16), jnp.full((16, 128), -1.0, BF16)], axis=0)

    def blank(flag, x_side):
        @pl.when(jnp.logical_not(flag))
        def _():
            edge = 0 if x_side == 0 else rows + 1
            pad[:, edge] = jnp.zeros((NSUB, lev, 128), F32)
            for ref in exs:
                ref[2 * rows * x_side : 2 * rows * x_side + rows] = zeros_ex
            wedge[x_side] = zeros_w
            wside[x_side] = zeros_w
            wcols[2 * x_side] = no_source
            wetn[x_side] = jnp.zeros((8, 128), jnp.int32)
            cp[:, 2 * x_side] = jnp.zeros((NSUB - 1, 2, 8, 128), F32)
            for k in range(8):
                eff_same[x_side, k] = -1
                eff_over[x_side, k] = -1

    blank(prev, 0)
    blank(nxt, 1)
    for x_side, flag in ((0, prev2), (1, nxt2)):

        @pl.when(jnp.logical_not(flag))
        def _():
            rp[:, x_side] = jnp.zeros((NSUB - 1, flux, 128), F32)

    for side, flag in ((0, left), (1, right)):

        @pl.when(jnp.logical_not(flag))
        def _():
            hz[:, side] = jnp.zeros((NSUB, 24, 128), F32)
            cp[:, :, side] = jnp.zeros((NSUB - 1, 3, 8, 128), F32)
            wets[side] = jnp.zeros((rows, 128), jnp.int32)

    for ref in exs:
        ref[3 * rows] = jnp.zeros((flux, 128), BF16)
    for ref in ess:
        ref[rows] = jnp.zeros((flux, 128), BF16)

    barrier = pltpu.get_barrier_semaphore()
    peers = [(None, over(0, 0))]
    peers += [(f, over(dx, 0)) for f, dx in ((prev, -1), (nxt, 1), (prev2, -2), (nxt2, 2))]
    peers += [(f, same(dx, 0)) for f, dx in ((prev, -1), (nxt, 1))]
    peers += [(f, same(0, dz)) for f, dz in ((left, -1), (right, 1))]
    peers += [
        (both(in_x[dx], f), over(dx, dz)) for dx in (-1, 0, 1) for f, dz in ((left, -1), (right, 1))
    ]
    expected = jnp.int32(0)
    for flag, peer in peers:
        when(
            flag,
            lambda peer=peer: pl.semaphore_signal(
                barrier, inc=1, device_id=peer, device_id_type=MESH
            ),
        )
        expected = expected + (1 if flag is None else flag.astype(jnp.int32))

    for copy in misc:
        copy.wait()
    ocean = c == 1
    wet[...] = jnp.where(ocean, weti[...].astype(F32), 1.0)
    rate[...] = rate[...] * wet[...]
    matrix = jnp.concatenate([ops[...], jnp.zeros((lev, 128 - lev), F32)], axis=1)
    high = matrix.astype(BF16).astype(F32)
    low = matrix - high
    lane = lane_ids((lev, 128))
    low80 = pltpu.roll(low, 80, 1)
    acat[...] = jnp.concatenate(
        [jnp.where(lane < 80, high, low80), jnp.where(lane < 32, low80, pltpu.roll(high, 32, 1))],
        axis=1,
    ).astype(BF16)
    acat16[...] = jnp.where(
        lane < flux,
        high,
        jnp.where(
            lane < 2 * flux,
            pltpu.roll(low, flux, 1),
            jnp.where(lane < 3 * flux, pltpu.roll(high, 2 * flux, 1), 0.0),
        ),
    ).astype(BF16)
    level = lax.broadcasted_iota(jnp.int32, (flux, 128), 0)
    scales = jnp.zeros((flux, 128), F32)
    gains = jnp.zeros((flux, 128), F32)
    for f in range(flux):
        scales = jnp.where(level == f, scale[0, f], scales)
        gains = jnp.where(level == f, gain[0, f], gains)

    def source_of(r, k):
        return jnp.where(k < count[0, 0, r], source[0, k, 0, r], -1)

    lane8 = lane_ids((8, 128))
    index = jnp.full((8, 128), -1, jnp.int32)
    for k in range(depth):
        for r in range(rows):
            index = jnp.where(lane8 // 2 == k * rows + r, source_of(r, k), index)
    index = index.astype(F32)
    for k in range(8):
        eff[k] = source_of(0 if k < 4 else rows - 1, k % 4) if k % 4 < depth else -1

    for copy in state_copies:
        copy.wait()

    def pack_edges(t):
        parts = [None] * 3
        for r in range(rows):
            for g in range(groups):
                slot, at = place(g, r)
                moved = pltpu.roll(pad[t, r + 1, 8 * g : 8 * g + 8, :], at + 1, 1)
                old = parts[slot]
                parts[slot] = moved if old is None else jnp.where(lane8 // 2 == at // 2, moved, old)
        zpack[t] = jnp.concatenate(parts, axis=0)

    pack_edges(0)

    pl.semaphore_wait(barrier, expected)

    ids = {}
    sent = []

    def remote(key, flag, src, dst, peer):
        at = ids.setdefault(key, len(ids))
        copy = pltpu.make_async_remote_copy(
            src_ref=src,
            dst_ref=dst,
            send_sem=send_sem.at[at],
            recv_sem=recv_sem.at[at],
            device_id=peer,
            device_id_type=MESH,
        )
        when(flag, copy.start)
        sent.append((flag, copy))

    def receive(key, flag, dst):
        at = ids[key]
        copy = pltpu.make_async_remote_copy(
            src_ref=dst,
            dst_ref=dst,
            send_sem=send_sem.at[at],
            recv_sem=recv_sem.at[at],
            device_id=over(0, 0),
            device_id_type=MESH,
        )
        when(flag, copy.wait_recv)

    def send_rows(first, last_row, t):
        remote(("hx", t, 0), nxt, last_row, pad.at[t, 0], same(1, 0))
        remote(("hx", t, 1), prev, first, pad.at[t, rows + 1], same(-1, 0))

    def send_columns(t):
        remote(("hz", t, 0), right, zpack.at[t], hz.at[t, 0], same(0, 1))
        remote(("hz", t, 1), left, zpack.at[t], hz.at[t, 1], same(0, -1))

    send_rows(fields.at[0, :, 0, :], fields.at[0, :, rows - 1, :], 0)
    send_columns(0)
    first, final_row = tiles.at[0, 0, 0], tiles.at[0, rows - 1, 0]
    remote("ws1", prev, final_row, wside.at[1], over(-1, 0))
    remote("ws0", nxt, first, wside.at[0], over(1, 0))
    remote("es0", nxt, eff, eff_same.at[0], same(1, 0))
    remote("es1", prev, eff, eff_same.at[1], same(-1, 0))
    remote("eo0", nxt, eff, eff_over.at[0], over(1, 0))
    remote("eo1", prev, eff, eff_over.at[1], over(-1, 0))
    remote("wn0", nxt, wetm.at[rows - 8 : rows], wetn.at[0], same(1, 0))
    remote("wn1", prev, wetm.at[0:8], wetn.at[1], same(-1, 0))
    remote("wz0", right, wetm, wets.at[0], same(0, 1))
    remote("wz1", left, wetm, wets.at[1], same(0, -1))

    tile_copy.wait()
    lane128 = lane_ids((128, 128))
    packed = jnp.zeros((128, 128), BF16)
    for k in range(depth):
        for r in range(rows):
            at = 2 * (k * rows + r)
            packed = jnp.where(lane128 // 2 == at // 2, pltpu.roll(w[r, k], at + 1, 1), packed)
    wcol[0:128] = packed
    wcol[128:144] = jnp.concatenate([index, index], axis=0).astype(BF16)
    for dx in (-1, 0, 1):
        remote(("wc", 1 - dx), in_x[dx], wcol, wcols.at[1 - dx], over(dx, 0))
    remote("we0", nxt, final_row, wedge.at[0], same(1, 0))
    remote("we1", prev, first, wedge.at[1], same(-1, 0))

    def merged_edges(t):
        odd = lane_ids((24, 128)) % 2 == 1
        return jnp.where(odd, hz[t, 1], hz[t, 0])

    def stencil(load, edges, n_groups, r):
        here = load(r + 1)
        levels = 8 * n_groups
        lane = lane_ids((levels, 128))
        moved = []
        for g in range(n_groups):
            slot, at = place(g, r)
            moved.append(pltpu.roll(edges[8 * slot : 8 * slot + 8], (127 - at) % 128, 1))
        beyond = jnp.concatenate(moved, axis=0)
        before = pltpu.roll(jnp.where(lane == 127, beyond, here), 1, 1)
        after = pltpu.roll(jnp.where(lane == 0, beyond, here), 127, 1)
        beside = load(r + 2) + load(r) + after + before
        return here + rate[r : r + 1, :] * (beside - 4.0 * here)

    def column_of(t, edges, some):
        for p in some:
            halves = []
            for r in (2 * p, 2 * p + 1):
                smooth = stencil(lambda i: pad[t, i], edges, groups, r)
                halves.append(
                    jnp.concatenate(split3(smooth, 80 - lev) + [jnp.zeros((16, 128), BF16)], axis=0)
                )
            product = jnp.dot(
                acat[...], jnp.concatenate(halves, axis=1), preferred_element_type=F32
            )
            ppre[2 * p] = product[:, :128]
            ppre[2 * p + 1] = product[:, 128:]

    def column_inner(t):
        receive(("hz", t, 0), left, hz.at[t, 0])
        receive(("hz", t, 1), right, hz.at[t, 1])
        column_of(t, merged_edges(t), range(1, pairs - 1))

    def column_outer(t):
        receive(("hx", t, 0), prev, pad.at[t, 0])
        receive(("hx", t, 1), nxt, pad.at[t, rows + 1])
        column_of(t, merged_edges(t), (0, pairs - 1))

    def pair_product(picks, weights):
        product = jnp.dot(
            jnp.concatenate([jnp.concatenate(row, axis=1) for row in picks], axis=0),
            jnp.concatenate([tile.reshape(depth * 128, 128) for tile in weights], axis=1),
            preferred_element_type=F32,
        )
        return product[:flux, :128], product[flux:, 128:]

    column_inner(0)
    column_outer(0)
    for t in range(NSUB):
        final = t == NSUB - 1
        col, at_col = (last, ()) if final else (pad, (t + 1,))

        def col_at(r):
            return (*at_col, r + (0 if final else 1))

        box, mine = exs[t], ess[t]
        for p in range(pairs):
            pair = [ppre[2 * p, 0:flux], ppre[2 * p + 1, 0:flux]]
            if t > 0:
                halves = []
                for r in (2 * p, 2 * p + 1):
                    smooth = stencil(lambda i: dpad[t - 1, i], dedges, fgroups, r)
                    halves.append(jnp.concatenate(split3(smooth, 0), axis=0))
                halves = jnp.concatenate(halves, axis=1)
                dsplit[p] = halves
                product = jnp.dot(acat16[0:flux, : 3 * flux], halves, preferred_element_type=F32)
                pair = [pair[0] + product[:, :128], pair[1] + product[:, 128:]]
            for i, r in enumerate((2 * p, 2 * p + 1)):
                mine[r] = (jnp.tanh(scales * pair[i]) * wet[r : r + 1, :]).astype(BF16)
                col[(*col_at(r), slice(0, flux))] = pair[i]
        block = mine.at[0:rows]
        remote(("ex", t, 0), nxt, block, box.at[0:rows], over(1, 0))
        remote(("ex", t, 2), prev, block, box.at[2 * rows : 3 * rows], over(-1, 0))
        remote(("ex", t, 1), None, block, box.at[rows : 2 * rows], over(0, 0))

        if not final:
            if t == 0:
                receive("ws0", prev, wside.at[0])
                receive("ws1", nxt, wside.at[1])
                receive("eo0", prev, eff_over.at[0])
                receive("eo1", nxt, eff_over.at[1])
            picks = [[], []]
            for k in range(depth):
                above, below = eff_over[0, k], eff_over[1, 4 + k]
                picks[0].append(mine[jnp.where(above >= 2 * rows, above - 2 * rows, rows)])
                picks[1].append(
                    mine[jnp.where(jnp.logical_and(below >= 0, below < rows), below, rows)]
                )
            parts = pair_product(picks, (wside[0], wside[1]))
            rpack[t, 0] = parts[0]
            rpack[t, 1] = parts[1]
            remote(("rp", t, 1), prev2, rpack.at[t, 0], rp.at[t, 1], over(-2, 0))
            remote(("rp", t, 0), nxt2, rpack.at[t, 1], rp.at[t, 0], over(2, 0))
            if t == 0:
                for dx in (-1, 0, 1):
                    receive(("wc", dx + 1), in_x[dx], wcols.at[dx + 1])
                    column, tag = wcols[dx + 1, 0:128], wcols[dx + 1, 128:144].astype(F32)[0:1]
                    for s in range(rows):
                        chosen = jnp.where(tag == float(rows * (1 - dx) + s), 1.0, 0.0).astype(BF16)
                        wd[s, :, 128 * (dx + 1) : 128 * (dx + 2)] = column * chosen
            product = jnp.dot(
                jnp.concatenate([mine[s] for s in range(rows)], axis=1),
                wd[...].reshape(rows * 128, 3 * 128),
                preferred_element_type=F32,
            )
            for dx in (-1, 0, 1):
                value = product[:, 128 * (dx + 1) : 128 * (dx + 2)]
                total = value
                for k in range(1, depth):
                    total = total + pltpu.roll(value, 128 - 2 * rows * k, 1)
                cpack[t, dx + 1] = jnp.where(
                    lane8 < 2 * rows, total[0:8], pltpu.roll(total[8:16], 2 * rows, 1)
                )
                for side, flag, dz in ((0, right, 1), (1, left, -1)):
                    remote(
                        ("cp", t, 1 - dx, side),
                        both(in_x[dx], flag),
                        cpack.at[t, dx + 1],
                        cp.at[t, 1 - dx, side],
                        over(dx, dz),
                    )

        if t > 0:
            for p in range(pairs):
                product = jnp.dot(
                    acat16[flux:, : 3 * flux], dsplit[p], preferred_element_type=F32
                )
                for i, r in enumerate((2 * p, 2 * p + 1)):
                    col[(*col_at(r), slice(flux, lev))] = (
                        ppre[r, flux:] + product[:, i * 128 : (i + 1) * 128]
                    )
        else:
            for r in range(rows):
                col[(*col_at(r), slice(flux, lev))] = ppre[r, flux:]

        if final:
            rest = [fetch(last.at[r, flux:], out.at[0, flux:, r, :]) for r in range(rows)]
        else:
            send_rows(pad.at[t + 1, 1], pad.at[t + 1, rows], t + 1)
            pack_edges(t + 1)
            send_columns(t + 1)
            column_inner(t + 1)

        receive(("ex", t, 1), None, box.at[rows : 2 * rows])
        receive(("ex", t, 0), prev, box.at[0:rows])
        receive(("ex", t, 2), nxt, box.at[2 * rows : 3 * rows])
        for p in range(pairs):
            picks = [[], []]
            for i in range(2):
                for k in range(depth):
                    at = source_of(2 * p + i, k)
                    picks[i].append(box[jnp.where(at >= 0, at, 3 * rows)])
            parts = pair_product(picks, (w[2 * p], w[2 * p + 1]))
            for i, r in enumerate((2 * p, 2 * p + 1)):
                value = gains * wet[r : r + 1, :] * parts[i]
                if final:
                    last[r, 0:flux] += value
                else:
                    dpad[t, r + 1] = value
        if final:
            top = [fetch(last.at[r, 0:flux], out.at[0, 0:flux, r, :]) for r in range(rows)]
        else:
            if t == 0:
                receive("es0", prev, eff_same.at[0])
                receive("es1", nxt, eff_same.at[1])
                receive("we0", prev, wedge.at[0])
                receive("we1", nxt, wedge.at[1])
                receive("wn0", prev, wetn.at[0])
                receive("wn1", nxt, wetn.at[1])
                receive("wz0", left, wets.at[0])
                receive("wz1", right, wets.at[1])
                wet_up = jnp.where(ocean, wetn[0, 7:8].astype(F32), 1.0)
                wet_down = jnp.where(ocean, wetn[1, 0:1].astype(F32), 1.0)
                beside = jnp.zeros((8, 128), F32)
                for r in range(rows):
                    for side, have in ((0, 127), (1, 0)):
                        at = 2 * r + side
                        cells = jnp.broadcast_to(wets[side, r : r + 1].astype(F32), (8, 128))
                        beside = jnp.where(
                            lane8 == at, pltpu.roll(cells, (at - have) % 128, 1), beside
                        )
                beside = jnp.where(ocean, beside, 1.0)
                gw[...] = jnp.where(
                    lane8 < 2 * rows,
                    beside * gains[0:8],
                    pltpu.roll(beside, 2 * rows, 1) * gains[8:16],
                )
            picks = [[], []]
            for k in range(depth):
                above, below = eff_same[0, 4 + k], eff_same[1, k]
                picks[0].append(box[jnp.where(above >= rows, above - rows, 3 * rows)])
                picks[1].append(
                    box[
                        jnp.where(
                            jnp.logical_and(below >= 0, below < 2 * rows), below + rows, 3 * rows
                        )
                    ]
                )
            parts = pair_product(picks, (wedge[0], wedge[1]))
            receive(("rp", t, 0), prev2, rp.at[t, 0])
            receive(("rp", t, 1), nxt2, rp.at[t, 1])
            dpad[t, 0] = gains * wet_up * (parts[0] + rp[t, 0])
            dpad[t, rows + 1] = gains * wet_down * (parts[1] + rp[t, 1])
            for dx in (-1, 0, 1):
                receive(("cp", t, dx + 1, 0), both(in_x[dx], left), cp.at[t, dx + 1, 0])
                receive(("cp", t, dx + 1, 1), both(in_x[dx], right), cp.at[t, dx + 1, 1])
            dedges = gw[...] * jnp.where(
                lane8 % 2 == 1,
                cp[t, 0, 1] + cp[t, 1, 1] + cp[t, 2, 1],
                cp[t, 0, 0] + cp[t, 1, 0] + cp[t, 2, 0],
            )
            column_outer(t + 1)

    for flag, copy in sent:
        when(flag, copy.wait_send)
    for copy in rest + top:
        copy.wait()


def on_device(*args):
    fields, export_scale, tile_source = args[0], args[4], args[6]
    _, lev, rows, width = fields.shape
    flux, depth = export_scale.shape[1], tile_source.shape[3]
    dma = pltpu.SemaphoreType.DMA
    any_ = pl.BlockSpec(memory_space=pl.ANY)
    smem = pl.BlockSpec(memory_space=pltpu.SMEM)
    vmem = pltpu.VMEM
    box = vmem((3 * rows + 1, flux, width), BF16)
    mine = vmem((rows + 1, flux, width), BF16)
    return pl.pallas_call(
        functools.partial(kernel, (lev, rows, flux, depth)),
        out_shape=jax.ShapeDtypeStruct(fields.shape, F32),
        in_specs=[any_, any_, any_, any_, smem, smem, smem, smem, any_],
        out_specs=any_,
        scratch_shapes=[
            vmem((NSUB, rows + 2, lev, width), F32),
            vmem((NSUB - 1, rows + 2, flux, width), F32),
            vmem((NSUB, 2, 24, width), F32),
            vmem((NSUB - 1, 3, 2, 8, width), F32),
            vmem((NSUB - 1, 2, flux, width), F32),
            vmem((rows, lev, width), F32),
            vmem((rows, lev, width), F32),
            vmem((NSUB, 24, width), F32),
            vmem((NSUB - 1, 3, 8, width), F32),
            vmem((NSUB - 1, 2, flux, width), F32),
            vmem((rows // 2, 3 * flux, 2 * width), BF16),
            vmem((rows, depth, width, width), BF16),
            vmem((2, depth, width, width), BF16),
            vmem((2, depth, width, width), BF16),
            vmem((144, width), BF16),
            vmem((3, 144, width), BF16),
            vmem((rows, width, 3 * width), BF16),
            vmem((rows, width), F32),
            vmem((rows, width), jnp.int32),
            vmem((rows, width), F32),
            vmem((2, 8, width), jnp.int32),
            vmem((2, rows, width), jnp.int32),
            vmem((8, width), F32),
            vmem((lev, lev), F32),
            vmem((lev, 256), BF16),
            vmem((lev, 128), BF16),
            box,
            box,
            box,
            box,
            mine,
            mine,
            mine,
            mine,
            pltpu.SMEM((8,), jnp.int32),
            pltpu.SMEM((2, 8), jnp.int32),
            pltpu.SMEM((2, 8), jnp.int32),
            dma((52,)),
            dma((80,)),
            dma((80,)),
        ],
        compiler_params=pltpu.CompilerParams(
            collective_id=0, has_side_effects=True, vmem_limit_bytes=56 * 1024 * 1024
        ),
        name="coupled",
    )(*args[:6], jnp.transpose(args[6], (0, 3, 2, 1)), jnp.transpose(args[7], (0, 2, 1)), args[8])


def solution(mesh):
    in_specs = (
        P("comp", None, "gx", "gz"),
        P("comp", "gx", "gz"),
        P("gx", "gz"),
        P("comp", None, None),
        P("comp", None),
        P("comp", None),
        P("comp", "gx", "gz", None),
        P("comp", "gx", "gz"),
        P("comp", "gx", "gz", None, None, None),
    )
    out_specs = P("comp", None, "gx", "gz")
    return jax.shard_map(
        on_device, mesh=mesh, in_specs=in_specs, out_specs=out_specs, check_vma=False
    )
```

```python
import functools

import jax
import jax.numpy as jnp
from jax import lax
from jax.experimental import pallas as pl
from jax.experimental.pallas import tpu as pltpu
from jax.sharding import PartitionSpec as P

NSUB = 4
MESH = pl.DeviceIdType.MESH
F32 = jnp.float32
BF16 = jnp.bfloat16


def lane_ids(shape):
    return lax.broadcasted_iota(jnp.int32, shape, 1)


def split3(value, pad):
    if pad:
        value = jnp.concatenate([value, jnp.zeros((pad, value.shape[1]), F32)], axis=0)
    high = value.astype(BF16)
    low = (value - high.astype(F32)).astype(BF16)
    return [high, high, low]


def place(group, row):
    return group // 4, 32 * (group % 4) + 2 * row


def kernel(dims, fields, diff, wetm, op, scale_in, gain_in, source_in, count_in, tiles, out, *scratch):
    lev, rows, flux, depth = dims
    last = out
    (pad, dpad, hz, cp, rp, ppre, hx, hxpack, zpack, cpack, rpack, dsplit, w, wedge, wcol, wcols, wd) = scratch[:17]
    (rate, weti, wet, wetn, wets, gw, ops, acat, acat16) = scratch[17:26]
    exs, ess = scratch[26:30], scratch[30:34]
    eff, eff_same, eff_over, scale, gain, source, count = scratch[34:41]
    local_sem, send_sem, recv_sem = scratch[41:44]
    groups, fgroups = lev // 8, flux // 8
    pairs = rows // 2
    c, gx, gz = lax.axis_index("comp"), lax.axis_index("gx"), lax.axis_index("gz")
    nx, nz = lax.axis_size("gx"), lax.axis_size("gz")
    prev, nxt, left, right = gx > 0, gx < nx - 1, gz > 0, gz < nz - 1
    prev2, nxt2 = gx > 1, gx < nx - 2

    def same(dx, dz):
        return (c, gx + dx, gz + dz)

    def over(dx, dz):
        return (1 - c, gx + dx, gz + dz)

    in_x = {-1: prev, 0: None, 1: nxt}

    def both(a, b):
        return b if a is None else a if b is None else jnp.logical_and(a, b)

    def when(flag, todo):
        if flag is None:
            todo()
        else:
            pl.when(flag)(todo)

    local = iter(range(100))

    def fetch(src, dst):
        copy = pltpu.make_async_copy(src, dst, local_sem.at[next(local)])
        copy.start()
        return copy

    zeros_w = jnp.zeros((depth, 128, 128), BF16)
    zeros_ex = jnp.zeros((rows, flux, 128), BF16)
    no_source = jnp.concatenate([jnp.zeros((128, 128), BF16), jnp.full((16, 128), -1.0, BF16)], axis=0)

    def blank(flag, x_side):
        @pl.when(jnp.logical_not(flag))
        def _():
            hx[:, x_side] = jnp.zeros((NSUB, 80, 128), BF16)
            for ref in exs:
                ref[2 * rows * x_side : 2 * rows * x_side + rows] = zeros_ex
            wedge[x_side] = zeros_w
            wcols[2 * x_side] = no_source
            wetn[x_side] = jnp.zeros((8, 128), jnp.int32)
            cp[:, 2 * x_side] = jnp.zeros((NSUB - 1, 2, 8, 128), F32)
            for k in range(8):
                eff_same[x_side, k] = -1
                eff_over[x_side, k] = -1

    blank(prev, 0)
    blank(nxt, 1)
    for x_side, flag in ((0, prev2), (1, nxt2)):

        @pl.when(jnp.logical_not(flag))
        def _():
            rp[:, x_side] = jnp.zeros((NSUB - 1, depth, flux, 128), BF16)

    for side, flag in ((0, left), (1, right)):

        @pl.when(jnp.logical_not(flag))
        def _():
            hz[:, side] = jnp.zeros((NSUB, 24, 128), F32)
            cp[:, :, side] = jnp.zeros((NSUB - 1, 3, 8, 128), F32)
            wets[side] = jnp.zeros((rows, 128), jnp.int32)

    for ref in exs:
        ref[3 * rows] = jnp.zeros((flux, 128), BF16)
    for ref in ess:
        ref[rows] = jnp.zeros((flux, 128), BF16)

    barrier = pltpu.get_barrier_semaphore()
    peers = [(None, over(0, 0))]
    peers += [(f, over(dx, 0)) for f, dx in ((prev, -1), (nxt, 1), (prev2, -2), (nxt2, 2))]
    peers += [(f, same(dx, 0)) for f, dx in ((prev, -1), (nxt, 1))]
    peers += [(f, same(0, dz)) for f, dz in ((left, -1), (right, 1))]
    peers += [
        (both(in_x[dx], f), over(dx, dz)) for dx in (-1, 0, 1) for f, dz in ((left, -1), (right, 1))
    ]
    expected = jnp.int32(0)
    for flag, peer in peers:
        when(
            flag,
            lambda peer=peer: pl.semaphore_signal(
                barrier, inc=1, device_id=peer, device_id_type=MESH
            ),
        )
        expected = expected + (1 if flag is None else flag.astype(jnp.int32))

    misc = [fetch(op.at[0], ops), fetch(diff.at[0], rate), fetch(wetm, weti)]
    misc += [fetch(scale_in, scale), fetch(gain_in, gain), fetch(source_in, source), fetch(count_in, count)]
    state_copies = [fetch(fields.at[0, :, r, :], pad.at[0, r + 1]) for r in range(rows)]
    tile_copy = fetch(tiles.at[0, :, 0], w)

    for copy in misc:
        copy.wait()
    ocean = c == 1
    wet[...] = jnp.where(ocean, weti[...].astype(F32), 1.0)
    rate[...] = rate[...] * wet[...]
    matrix = jnp.concatenate([ops[...], jnp.zeros((lev, 128 - lev), F32)], axis=1)
    high = matrix.astype(BF16).astype(F32)
    low = matrix - high
    lane = lane_ids((lev, 128))
    low80 = pltpu.roll(low, 80, 1)
    acat[...] = jnp.concatenate(
        [jnp.where(lane < 80, high, low80), jnp.where(lane < 32, low80, pltpu.roll(high, 32, 1))],
        axis=1,
    ).astype(BF16)
    acat16[...] = jnp.where(
        lane < flux,
        high,
        jnp.where(
            lane < 2 * flux,
            pltpu.roll(low, flux, 1),
            jnp.where(lane < 3 * flux, pltpu.roll(high, 2 * flux, 1), 0.0),
        ),
    ).astype(BF16)
    level = lax.broadcasted_iota(jnp.int32, (flux, 128), 0)
    scales = jnp.zeros((flux, 128), F32)
    gains = jnp.zeros((flux, 128), F32)
    for f in range(flux):
        scales = jnp.where(level == f, scale[0, f], scales)
        gains = jnp.where(level == f, gain[0, f], gains)

    def source_of(r, k):
        return jnp.where(k < count[0, 0, r], source[0, k, 0, r], -1)

    lane8 = lane_ids((8, 128))
    index = jnp.full((8, 128), -1, jnp.int32)
    for k in range(depth):
        for r in range(rows):
            index = jnp.where(lane8 // 2 == k * rows + r, source_of(r, k), index)
    index = index.astype(F32)
    for k in range(8):
        eff[k] = source_of(0 if k < 4 else rows - 1, k % 4) if k % 4 < depth else -1

    for copy in state_copies:
        copy.wait()

    def pack_edges(t):
        parts = [None] * 3
        for r in range(rows):
            for g in range(groups):
                slot, at = place(g, r)
                moved = pltpu.roll(pad[t, r + 1, 8 * g : 8 * g + 8, :], at + 1, 1)
                old = parts[slot]
                parts[slot] = moved if old is None else jnp.where(lane8 // 2 == at // 2, moved, old)
        zpack[t] = jnp.concatenate(parts, axis=0)

    def pack_rows(t):
        for i, at in enumerate((rows, 1)):
            hxpack[t, i] = jnp.concatenate([pad[t, at], jnp.zeros((80 - lev, 128), F32)], axis=0).astype(BF16)

    pack_rows(0)
    pack_edges(0)

    pl.semaphore_wait(barrier, expected)

    ids = {}
    sent = []

    def remote(key, flag, src, dst, peer):
        at = ids.setdefault(key, len(ids))
        copy = pltpu.make_async_remote_copy(
            src_ref=src,
            dst_ref=dst,
            send_sem=send_sem.at[at],
            recv_sem=recv_sem.at[at],
            device_id=peer,
            device_id_type=MESH,
        )
        when(flag, copy.start)
        sent.append((flag, copy))

    def receive(key, flag, dst):
        at = ids[key]
        copy = pltpu.make_async_remote_copy(
            src_ref=dst,
            dst_ref=dst,
            send_sem=send_sem.at[at],
            recv_sem=recv_sem.at[at],
            device_id=over(0, 0),
            device_id_type=MESH,
        )
        when(flag, copy.wait_recv)

    def send_rows(t):
        remote(("hx", t, 0), nxt, hxpack.at[t, 0], hx.at[t, 0], same(1, 0))
        remote(("hx", t, 1), prev, hxpack.at[t, 1], hx.at[t, 1], same(-1, 0))

    def send_columns(t):
        remote(("hz", t, 0), right, zpack.at[t], hz.at[t, 0], same(0, 1))
        remote(("hz", t, 1), left, zpack.at[t], hz.at[t, 1], same(0, -1))

    send_rows(0)
    send_columns(0)
    first, final_row = tiles.at[0, 0, 0], tiles.at[0, rows - 1, 0]
    remote("es0", nxt, eff, eff_same.at[0], same(1, 0))
    remote("es1", prev, eff, eff_same.at[1], same(-1, 0))
    remote("eo0", nxt, eff, eff_over.at[0], over(1, 0))
    remote("eo1", prev, eff, eff_over.at[1], over(-1, 0))
    remote("wn0", nxt, wetm.at[rows - 8 : rows], wetn.at[0], same(1, 0))
    remote("wn1", prev, wetm.at[0:8], wetn.at[1], same(-1, 0))
    remote("wz0", right, wetm, wets.at[0], same(0, 1))
    remote("wz1", left, wetm, wets.at[1], same(0, -1))

    tile_copy.wait()
    lane128 = lane_ids((128, 128))
    packed = jnp.zeros((128, 128), BF16)
    for k in range(depth):
        for r in range(rows):
            at = 2 * (k * rows + r)
            packed = jnp.where(lane128 // 2 == at // 2, pltpu.roll(w[r, k], at + 1, 1), packed)
    wcol[0:128] = packed
    wcol[128:144] = jnp.concatenate([index, index], axis=0).astype(BF16)
    for dx in (-1, 0, 1):
        remote(("wc", 1 - dx), in_x[dx], wcol, wcols.at[1 - dx], over(dx, 0))
    remote("we0", nxt, final_row, wedge.at[0], same(1, 0))
    remote("we1", prev, first, wedge.at[1], same(-1, 0))

    def merged_edges(t):
        odd = lane_ids((24, 128)) % 2 == 1
        return jnp.where(odd, hz[t, 1], hz[t, 0])

    def stencil(load, edges, n_groups, r):
        here = load(r + 1)
        levels = 8 * n_groups
        lane = lane_ids((levels, 128))
        moved = []
        for g in range(n_groups):
            slot, at = place(g, r)
            moved.append(pltpu.roll(edges[8 * slot : 8 * slot + 8], (127 - at) % 128, 1))
        beyond = jnp.concatenate(moved, axis=0)
        before = pltpu.roll(jnp.where(lane == 127, beyond, here), 1, 1)
        after = pltpu.roll(jnp.where(lane == 0, beyond, here), 127, 1)
        beside = load(r + 2) + load(r) + after + before
        return here + rate[r : r + 1, :] * (beside - 4.0 * here)

    def column_of(t, edges, some):
        def row_of(i):
            if i in (0, rows + 1):
                return hx[t, min(i, 1)].astype(F32)[:lev]
            return pad[t, i]

        for p in some:
            halves = []
            for r in (2 * p, 2 * p + 1):
                smooth = stencil(row_of, edges, groups, r)
                halves.append(
                    jnp.concatenate(split3(smooth, 80 - lev) + [jnp.zeros((16, 128), BF16)], axis=0)
                )
            product = jnp.dot(
                acat[...], jnp.concatenate(halves, axis=1), preferred_element_type=F32
            )
            ppre[2 * p] = product[:, :128]
            ppre[2 * p + 1] = product[:, 128:]

    def column_inner(t):
        receive(("hz", t, 0), left, hz.at[t, 0])
        receive(("hz", t, 1), right, hz.at[t, 1])
        column_of(t, merged_edges(t), range(1, pairs - 1))

    def column_outer(t):
        receive(("hx", t, 0), prev, hx.at[t, 0])
        receive(("hx", t, 1), nxt, hx.at[t, 1])
        column_of(t, merged_edges(t), (0, pairs - 1))

    def pair_product(picks, weights):
        product = jnp.dot(
            jnp.concatenate([jnp.concatenate(row, axis=1) for row in picks], axis=0),
            jnp.concatenate([tile.reshape(depth * 128, 128) for tile in weights], axis=1),
            preferred_element_type=F32,
        )
        return product[:flux, :128], product[flux:, 128:]

    def send_parts(t):
        if t == 0:
            for dx in (-1, 0, 1):
                receive(("wc", dx + 1), in_x[dx], wcols.at[dx + 1])
                column, tag = wcols[dx + 1, 0:128], wcols[dx + 1, 128:144].astype(F32)[0:1]
                for s in range(rows):
                    chosen = jnp.where(tag == float(rows * (1 - dx) + s), 1.0, 0.0).astype(BF16)
                    wd[s, :, 128 * (dx + 1) : 128 * (dx + 2)] = column * chosen
        product = jnp.dot(
            jnp.concatenate([ess[t][s] for s in range(rows)], axis=1),
            wd[...].reshape(rows * 128, 3 * 128),
            preferred_element_type=F32,
        )
        for dx in (-1, 0, 1):
            value = product[:, 128 * (dx + 1) : 128 * (dx + 2)]
            total = value
            for k in range(1, depth):
                total = total + pltpu.roll(value, 128 - 2 * rows * k, 1)
            cpack[t, dx + 1] = jnp.where(
                lane8 < 2 * rows, total[0:8], pltpu.roll(total[8:16], 2 * rows, 1)
            )
            for side, flag, dz in ((0, right, 1), (1, left, -1)):
                remote(
                    ("cp", t, 1 - dx, side),
                    both(in_x[dx], flag),
                    cpack.at[t, dx + 1],
                    cp.at[t, 1 - dx, side],
                    over(dx, dz),
                )

    column_inner(0)
    column_outer(0)
    for t in range(NSUB):
        final = t == NSUB - 1
        col, at_col = (last, ()) if final else (pad, (t + 1,))

        def col_at(r):
            return (*at_col, r + (0 if final else 1))

        box, mine = exs[t], ess[t]
        for p in range(pairs):
            pair = [ppre[2 * p, 0:flux], ppre[2 * p + 1, 0:flux]]
            if t > 0:
                halves = []
                for r in (2 * p, 2 * p + 1):
                    smooth = stencil(lambda i: dpad[t - 1, i], dedges, fgroups, r)
                    halves.append(jnp.concatenate(split3(smooth, 0), axis=0))
                halves = jnp.concatenate(halves, axis=1)
                dsplit[p] = halves
                product = jnp.dot(acat16[0:flux, : 3 * flux], halves, preferred_element_type=F32)
                pair = [pair[0] + product[:, :128], pair[1] + product[:, 128:]]
            for i, r in enumerate((2 * p, 2 * p + 1)):
                mine[r] = (jnp.tanh(scales * pair[i]) * wet[r : r + 1, :]).astype(BF16)
                col[(*col_at(r), slice(0, flux))] = pair[i]
        block = mine.at[0:rows]
        remote(("ex", t, 0), nxt, block, box.at[0:rows], over(1, 0))
        remote(("ex", t, 2), prev, block, box.at[2 * rows : 3 * rows], over(-1, 0))
        remote(("ex", t, 1), None, block, box.at[rows : 2 * rows], over(0, 0))

        if not final:
            if t == 0:
                receive("eo0", prev, eff_over.at[0])
                receive("eo1", nxt, eff_over.at[1])
            for k in range(depth):
                above, below = eff_over[0, k], eff_over[1, 4 + k]
                rpack[t, 0, k] = mine[jnp.where(above >= 2 * rows, above - 2 * rows, rows)]
                rpack[t, 1, k] = mine[jnp.where(jnp.logical_and(below >= 0, below < rows), below, rows)]
            remote(("rp", t, 1), prev2, rpack.at[t, 0], rp.at[t, 1], over(-2, 0))
            remote(("rp", t, 0), nxt2, rpack.at[t, 1], rp.at[t, 0], over(2, 0))

        if 0 < t < NSUB - 1:
            send_parts(t)
        if t > 0:
            for p in range(pairs):
                product = jnp.dot(
                    acat16[flux:, : 3 * flux], dsplit[p], preferred_element_type=F32
                )
                for i, r in enumerate((2 * p, 2 * p + 1)):
                    col[(*col_at(r), slice(flux, lev))] = (
                        ppre[r, flux:] + product[:, i * 128 : (i + 1) * 128]
                    )
        else:
            for r in range(rows):
                col[(*col_at(r), slice(flux, lev))] = ppre[r, flux:]

        if not final:
            pack_rows(t + 1)
            send_rows(t + 1)
            pack_edges(t + 1)
            send_columns(t + 1)
            if t == 0:
                send_parts(0)
            column_inner(t + 1)

        receive(("ex", t, 1), None, box.at[rows : 2 * rows])
        receive(("ex", t, 0), prev, box.at[0:rows])
        receive(("ex", t, 2), nxt, box.at[2 * rows : 3 * rows])
        for p in range(pairs):
            picks = [[], []]
            for i in range(2):
                for k in range(depth):
                    at = source_of(2 * p + i, k)
                    picks[i].append(box[jnp.where(at >= 0, at, 3 * rows)])
            parts = pair_product(picks, (w[2 * p], w[2 * p + 1]))
            for i, r in enumerate((2 * p, 2 * p + 1)):
                value = gains * wet[r : r + 1, :] * parts[i]
                if final:
                    last[r, 0:flux] += value
                else:
                    dpad[t, r + 1] = value
        if not final:
            if t == 0:
                receive("es0", prev, eff_same.at[0])
                receive("es1", nxt, eff_same.at[1])
                receive("we0", prev, wedge.at[0])
                receive("we1", nxt, wedge.at[1])
                receive("wn0", prev, wetn.at[0])
                receive("wn1", nxt, wetn.at[1])
                receive("wz0", left, wets.at[0])
                receive("wz1", right, wets.at[1])
                wet_up = jnp.where(ocean, wetn[0, 7:8].astype(F32), 1.0)
                wet_down = jnp.where(ocean, wetn[1, 0:1].astype(F32), 1.0)
                beside = jnp.zeros((8, 128), F32)
                for r in range(rows):
                    for side, have in ((0, 127), (1, 0)):
                        at = 2 * r + side
                        cells = jnp.broadcast_to(wets[side, r : r + 1].astype(F32), (8, 128))
                        beside = jnp.where(
                            lane8 == at, pltpu.roll(cells, (at - have) % 128, 1), beside
                        )
                beside = jnp.where(ocean, beside, 1.0)
                gw[...] = jnp.where(
                    lane8 < 2 * rows,
                    beside * gains[0:8],
                    pltpu.roll(beside, 2 * rows, 1) * gains[8:16],
                )
            receive(("rp", t, 0), prev2, rp.at[t, 0])
            receive(("rp", t, 1), nxt2, rp.at[t, 1])
            picks = [[], []]
            for k in range(depth):
                above, below = eff_same[0, 4 + k], eff_same[1, k]
                here = jnp.where(above >= rows, above - rows, 3 * rows)
                picks[0].append(box[here] + rp[t, 0, k])
                here = jnp.where(jnp.logical_and(below >= 0, below < 2 * rows), below + rows, 3 * rows)
                picks[1].append(box[here] + rp[t, 1, k])
            parts = pair_product(picks, (wedge[0], wedge[1]))
            dpad[t, 0] = gains * wet_up * parts[0]
            dpad[t, rows + 1] = gains * wet_down * parts[1]
            for dx in (-1, 0, 1):
                receive(("cp", t, dx + 1, 0), both(in_x[dx], left), cp.at[t, dx + 1, 0])
                receive(("cp", t, dx + 1, 1), both(in_x[dx], right), cp.at[t, dx + 1, 1])
            dedges = gw[...] * jnp.where(
                lane8 % 2 == 1,
                cp[t, 0, 1] + cp[t, 1, 1] + cp[t, 2, 1],
                cp[t, 0, 0] + cp[t, 1, 0] + cp[t, 2, 0],
            )
            column_outer(t + 1)

    for flag, copy in sent:
        when(flag, copy.wait_send)


def on_device(*args):
    fields, export_scale, tile_source = args[0], args[4], args[6]
    _, lev, rows, width = fields.shape
    flux, depth = export_scale.shape[1], tile_source.shape[3]
    dma = pltpu.SemaphoreType.DMA
    any_ = pl.BlockSpec(memory_space=pl.ANY)
    vmem = pltpu.VMEM
    box = vmem((3 * rows + 1, flux, width), BF16)
    mine = vmem((rows + 1, flux, width), BF16)
    result = pl.pallas_call(
        functools.partial(kernel, (lev, rows, flux, depth)),
        out_shape=pltpu.VMEM((rows, lev, width), F32),
        in_specs=[any_] * 9,
        out_specs=pl.BlockSpec(memory_space=pltpu.VMEM),
        scratch_shapes=[
            vmem((NSUB, rows + 2, lev, width), F32),
            vmem((NSUB - 1, rows + 2, flux, width), F32),
            vmem((NSUB, 2, 24, width), F32),
            vmem((NSUB - 1, 3, 2, 8, width), F32),
            vmem((NSUB - 1, 2, depth, flux, width), BF16),
            vmem((rows, lev, width), F32),
            vmem((NSUB, 2, 80, width), BF16),
            vmem((NSUB, 2, 80, width), BF16),
            vmem((NSUB, 24, width), F32),
            vmem((NSUB - 1, 3, 8, width), F32),
            vmem((NSUB - 1, 2, depth, flux, width), BF16),
            vmem((rows // 2, 3 * flux, 2 * width), BF16),
            vmem((rows, depth, width, width), BF16),
            vmem((2, depth, width, width), BF16),
            vmem((144, width), BF16),
            vmem((3, 144, width), BF16),
            vmem((rows, width, 3 * width), BF16),
            vmem((rows, width), F32),
            vmem((rows, width), jnp.int32),
            vmem((rows, width), F32),
            vmem((2, 8, width), jnp.int32),
            vmem((2, rows, width), jnp.int32),
            vmem((8, width), F32),
            vmem((lev, lev), F32),
            vmem((lev, 256), BF16),
            vmem((lev, 128), BF16),
            box,
            box,
            box,
            box,
            mine,
            mine,
            mine,
            mine,
            pltpu.SMEM((8,), jnp.int32),
            pltpu.SMEM((2, 8), jnp.int32),
            pltpu.SMEM((2, 8), jnp.int32),
            pltpu.SMEM((1, flux), F32),
            pltpu.SMEM((1, flux), F32),
            pltpu.SMEM((1, depth, 1, rows), jnp.int32),
            pltpu.SMEM((1, 1, rows), jnp.int32),
            dma((24,)),
            dma((80,)),
            dma((80,)),
        ],
        compiler_params=pltpu.CompilerParams(
            collective_id=0, has_side_effects=True, vmem_limit_bytes=56 * 1024 * 1024
        ),
        name="coupled",
    )(*args[:6], jnp.transpose(args[6], (0, 3, 2, 1)), jnp.transpose(args[7], (0, 2, 1)), args[8])
    return jnp.transpose(result, (1, 0, 2))[None]


def solution(mesh):
    in_specs = (
        P("comp", None, "gx", "gz"),
        P("comp", "gx", "gz"),
        P("gx", "gz"),
        P("comp", None, None),
        P("comp", None),
        P("comp", None),
        P("comp", "gx", "gz", None),
        P("comp", "gx", "gz"),
        P("comp", "gx", "gz", None, None, None),
    )
    out_specs = P("comp", None, "gx", "gz")
    return jax.shard_map(
        on_device, mesh=mesh, in_specs=in_specs, out_specs=out_specs, check_vma=False
    )
```

```python
import functools

import jax
import jax.numpy as jnp
from jax import lax
from jax.experimental import pallas as pl
from jax.experimental.pallas import tpu as pltpu
from jax.sharding import PartitionSpec as P

NSUB = 4
MESH = pl.DeviceIdType.MESH
F32 = jnp.float32
BF16 = jnp.bfloat16


def lane_ids(shape):
    return lax.broadcasted_iota(jnp.int32, shape, 1)


def split3(value, pad):
    if pad:
        value = jnp.concatenate([value, jnp.zeros((pad, value.shape[1]), F32)], axis=0)
    high = value.astype(BF16)
    low = (value - high.astype(F32)).astype(BF16)
    return [high, high, low]


def place(group, row):
    return group // 4, 32 * (group % 4) + 2 * row


def kernel(dims, fields, diff, wetm, op, scale_in, gain_in, source_in, count_in, tiles, out, *scratch):
    lev, rows, flux, depth = dims
    last = out
    (pad, dpad, hz, cp, rp, ppre, hx, hxpack, zpack, cpack, rpack, dsplit, w, wedge, wcol, wcols, wd) = scratch[:17]
    (rate, weti, wet, wetn, wets, gw, ops, acat, acat16) = scratch[17:26]
    exs, ess = scratch[26:30], scratch[30:34]
    eff, eff_same, eff_over, scale, gain, source, count = scratch[34:41]
    local_sem, send_sem, recv_sem = scratch[41:44]
    groups, fgroups = lev // 8, flux // 8
    pairs = rows // 2
    c, gx, gz = lax.axis_index("comp"), lax.axis_index("gx"), lax.axis_index("gz")
    nx, nz = lax.axis_size("gx"), lax.axis_size("gz")
    prev, nxt, left, right = gx > 0, gx < nx - 1, gz > 0, gz < nz - 1
    prev2, nxt2 = gx > 1, gx < nx - 2

    def same(dx, dz):
        return (c, gx + dx, gz + dz)

    def over(dx, dz):
        return (1 - c, gx + dx, gz + dz)

    in_x = {-1: prev, 0: None, 1: nxt}

    def both(a, b):
        return b if a is None else a if b is None else jnp.logical_and(a, b)

    def when(flag, todo):
        if flag is None:
            todo()
        else:
            pl.when(flag)(todo)

    local = iter(range(100))

    def fetch(src, dst):
        copy = pltpu.make_async_copy(src, dst, local_sem.at[next(local)])
        copy.start()
        return copy

    zeros_w = jnp.zeros((depth, 128, 128), BF16)
    zeros_ex = jnp.zeros((rows, flux, 128), BF16)
    no_source = jnp.concatenate([jnp.zeros((128, 128), BF16), jnp.full((16, 128), -1.0, BF16)], axis=0)

    def blank(flag, x_side):
        @pl.when(jnp.logical_not(flag))
        def _():
            hx[:, x_side] = jnp.zeros((NSUB, 80, 128), BF16)
            for ref in exs:
                ref[2 * rows * x_side : 2 * rows * x_side + rows] = zeros_ex
            wedge[x_side] = zeros_w
            wcols[2 * x_side] = no_source
            wetn[x_side] = jnp.zeros((8, 128), jnp.int32)
            cp[:, 2 * x_side] = jnp.zeros((NSUB - 1, 2, 8, 128), F32)
            for k in range(8):
                eff_same[x_side, k] = -1
                eff_over[x_side, k] = -1

    blank(prev, 0)
    blank(nxt, 1)
    for x_side, flag in ((0, prev2), (1, nxt2)):

        @pl.when(jnp.logical_not(flag))
        def _():
            rp[:, x_side] = jnp.zeros((NSUB - 1, depth, flux, 128), BF16)

    for side, flag in ((0, left), (1, right)):

        @pl.when(jnp.logical_not(flag))
        def _():
            hz[:, side] = jnp.zeros((NSUB, 24, 128), F32)
            cp[:, :, side] = jnp.zeros((NSUB - 1, 3, 8, 128), F32)
            wets[side] = jnp.zeros((rows, 128), jnp.int32)

    for ref in exs:
        ref[3 * rows] = jnp.zeros((flux, 128), BF16)
    for ref in ess:
        ref[rows] = jnp.zeros((flux, 128), BF16)

    barrier = pltpu.get_barrier_semaphore()
    peers = [(None, over(0, 0))]
    peers += [(f, over(dx, 0)) for f, dx in ((prev, -1), (nxt, 1))]
    peers += [(f, same(dx, 0)) for f, dx in ((prev, -1), (nxt, 1))]
    peers += [(f, same(0, dz)) for f, dz in ((left, -1), (right, 1))]
    expected = jnp.int32(0)
    for flag, peer in peers:
        when(
            flag,
            lambda peer=peer: pl.semaphore_signal(
                barrier, inc=1, device_id=peer, device_id_type=MESH
            ),
        )
        expected = expected + (1 if flag is None else flag.astype(jnp.int32))

    misc = [fetch(op.at[0], ops), fetch(diff.at[0], rate), fetch(wetm, weti)]
    misc += [fetch(scale_in, scale), fetch(gain_in, gain), fetch(source_in, source), fetch(count_in, count)]
    state_copies = [fetch(fields.at[0, :, r, :], pad.at[0, r + 1]) for r in range(rows)]
    tile_copy = fetch(tiles.at[0, :, 0], w)

    for copy in misc:
        copy.wait()
    ocean = c == 1
    wet[...] = jnp.where(ocean, weti[...].astype(F32), 1.0)
    rate[...] = rate[...] * wet[...]
    matrix = jnp.concatenate([ops[...], jnp.zeros((lev, 128 - lev), F32)], axis=1)
    high = matrix.astype(BF16).astype(F32)
    low = matrix - high
    lane = lane_ids((lev, 128))
    low80 = pltpu.roll(low, 80, 1)
    acat[...] = jnp.concatenate(
        [jnp.where(lane < 80, high, low80), jnp.where(lane < 32, low80, pltpu.roll(high, 32, 1))],
        axis=1,
    ).astype(BF16)
    acat16[...] = jnp.where(
        lane < flux,
        high,
        jnp.where(
            lane < 2 * flux,
            pltpu.roll(low, flux, 1),
            jnp.where(lane < 3 * flux, pltpu.roll(high, 2 * flux, 1), 0.0),
        ),
    ).astype(BF16)
    level = lax.broadcasted_iota(jnp.int32, (flux, 128), 0)
    scales = jnp.zeros((flux, 128), F32)
    gains = jnp.zeros((flux, 128), F32)
    for f in range(flux):
        scales = jnp.where(level == f, scale[0, f], scales)
        gains = jnp.where(level == f, gain[0, f], gains)

    def source_of(r, k):
        return jnp.where(k < count[0, 0, r], source[0, k, 0, r], -1)

    lane8 = lane_ids((8, 128))
    index = jnp.full((8, 128), -1, jnp.int32)
    for k in range(depth):
        for r in range(rows):
            index = jnp.where(lane8 // 2 == k * rows + r, source_of(r, k), index)
    index = index.astype(F32)
    for k in range(8):
        eff[k] = source_of(0 if k < 4 else rows - 1, k % 4) if k % 4 < depth else -1

    for copy in state_copies:
        copy.wait()

    def pack_edges(t):
        parts = [None] * 3
        for r in range(rows):
            for g in range(groups):
                slot, at = place(g, r)
                moved = pltpu.roll(pad[t, r + 1, 8 * g : 8 * g + 8, :], at + 1, 1)
                old = parts[slot]
                parts[slot] = moved if old is None else jnp.where(lane8 // 2 == at // 2, moved, old)
        zpack[t] = jnp.concatenate(parts, axis=0)

    def pack_rows(t):
        for i, at in enumerate((rows, 1)):
            hxpack[t, i] = jnp.concatenate([pad[t, at], jnp.zeros((80 - lev, 128), F32)], axis=0).astype(BF16)

    pack_rows(0)
    pack_edges(0)

    pl.semaphore_wait(barrier, expected)

    ids = {}
    sent = []

    def remote(key, flag, src, dst, peer):
        at = ids.setdefault(key, len(ids))
        copy = pltpu.make_async_remote_copy(
            src_ref=src,
            dst_ref=dst,
            send_sem=send_sem.at[at],
            recv_sem=recv_sem.at[at],
            device_id=peer,
            device_id_type=MESH,
        )
        when(flag, copy.start)
        sent.append((flag, copy))

    def receive(key, flag, dst):
        at = ids[key]
        copy = pltpu.make_async_remote_copy(
            src_ref=dst,
            dst_ref=dst,
            send_sem=send_sem.at[at],
            recv_sem=recv_sem.at[at],
            device_id=over(0, 0),
            device_id_type=MESH,
        )
        when(flag, copy.wait_recv)

    def send_rows(t):
        remote(("hx", t, 0), nxt, hxpack.at[t, 0], hx.at[t, 0], same(1, 0))
        remote(("hx", t, 1), prev, hxpack.at[t, 1], hx.at[t, 1], same(-1, 0))

    def send_columns(t):
        remote(("hz", t, 0), right, zpack.at[t], hz.at[t, 0], same(0, 1))
        remote(("hz", t, 1), left, zpack.at[t], hz.at[t, 1], same(0, -1))

    send_rows(0)
    send_columns(0)
    first, final_row = tiles.at[0, 0, 0], tiles.at[0, rows - 1, 0]
    remote("es0", nxt, eff, eff_same.at[0], same(1, 0))
    remote("es1", prev, eff, eff_same.at[1], same(-1, 0))
    remote("eo0", nxt, eff, eff_over.at[0], over(1, 0))
    remote("eo1", prev, eff, eff_over.at[1], over(-1, 0))
    remote("wn0", nxt, wetm.at[rows - 8 : rows], wetn.at[0], same(1, 0))
    remote("wn1", prev, wetm.at[0:8], wetn.at[1], same(-1, 0))
    remote("wz0", right, wetm, wets.at[0], same(0, 1))
    remote("wz1", left, wetm, wets.at[1], same(0, -1))

    tile_copy.wait()
    lane128 = lane_ids((128, 128))
    packed = jnp.zeros((128, 128), BF16)
    for k in range(depth):
        for r in range(rows):
            at = 2 * (k * rows + r)
            packed = jnp.where(lane128 // 2 == at // 2, pltpu.roll(w[r, k], at + 1, 1), packed)
    wcol[0:128] = packed
    wcol[128:144] = jnp.concatenate([index, index], axis=0).astype(BF16)
    for dx in (-1, 0, 1):
        remote(("wc", 1 - dx), in_x[dx], wcol, wcols.at[1 - dx], over(dx, 0))
    remote("we0", nxt, final_row, wedge.at[0], same(1, 0))
    remote("we1", prev, first, wedge.at[1], same(-1, 0))

    def merged_edges(t):
        odd = lane_ids((24, 128)) % 2 == 1
        return jnp.where(odd, hz[t, 1], hz[t, 0])

    def stencil(load, edges, n_groups, r):
        here = load(r + 1)
        levels = 8 * n_groups
        lane = lane_ids((levels, 128))
        moved = []
        for g in range(n_groups):
            slot, at = place(g, r)
            moved.append(pltpu.roll(edges[8 * slot : 8 * slot + 8], (127 - at) % 128, 1))
        beyond = jnp.concatenate(moved, axis=0)
        before = pltpu.roll(jnp.where(lane == 127, beyond, here), 1, 1)
        after = pltpu.roll(jnp.where(lane == 0, beyond, here), 127, 1)
        beside = load(r + 2) + load(r) + after + before
        return here + rate[r : r + 1, :] * (beside - 4.0 * here)

    def column_of(t, edges, some):
        def row_of(i):
            if i in (0, rows + 1):
                return hx[t, min(i, 1)].astype(F32)[:lev]
            return pad[t, i]

        for p in some:
            halves = []
            for r in (2 * p, 2 * p + 1):
                smooth = stencil(row_of, edges, groups, r)
                halves.append(
                    jnp.concatenate(split3(smooth, 80 - lev) + [jnp.zeros((16, 128), BF16)], axis=0)
                )
            product = jnp.dot(
                acat[...], jnp.concatenate(halves, axis=1), preferred_element_type=F32
            )
            ppre[2 * p] = product[:, :128]
            ppre[2 * p + 1] = product[:, 128:]

    def column_inner(t):
        receive(("hz", t, 0), left, hz.at[t, 0])
        receive(("hz", t, 1), right, hz.at[t, 1])
        column_of(t, merged_edges(t), range(1, pairs - 1))

    def column_outer(t):
        receive(("hx", t, 0), prev, hx.at[t, 0])
        receive(("hx", t, 1), nxt, hx.at[t, 1])
        column_of(t, merged_edges(t), (0, pairs - 1))

    def pair_product(picks, weights):
        product = jnp.dot(
            jnp.concatenate([jnp.concatenate(row, axis=1) for row in picks], axis=0),
            jnp.concatenate([tile.reshape(depth * 128, 128) for tile in weights], axis=1),
            preferred_element_type=F32,
        )
        return product[:flux, :128], product[flux:, 128:]

    def spread_columns():
        group = lane128 // (2 * rows)
        group8 = lane8 // (2 * rows)
        for dx in (-1, 0, 1):
            receive(("wc", dx + 1), in_x[dx], wcols.at[dx + 1])
        tags, columns = [], []
        for k in range(depth):
            tag = jnp.full((8, 128), -1.0, F32)
            column = jnp.zeros((128, 128), BF16)
            for dx in (-1, 0, 1):
                shift = (2 * rows * (dx + 1 - k)) % 128
                moved, own = wcols[dx + 1, 0:128], wcols[dx + 1, 128:144].astype(F32)[0:8]
                if shift:
                    moved, own = pltpu.roll(moved, shift, 1), pltpu.roll(own, shift, 1)
                tag = jnp.where(group8 == dx + 1, own - float(rows * (1 - dx)), tag)
                column = jnp.where(group == dx + 1, moved, column)
            tags.append(tag[0:1])
            columns.append(column)
        for row in range(rows):
            total = None
            for k in range(depth):
                term = columns[k] * jnp.where(tags[k] == float(row), 1.0, 0.0).astype(BF16)
                total = term if total is None else total + term
            wd[row] = total

    def send_parts(t, exported):
        value = jnp.dot(
            jnp.concatenate(exported, axis=1),
            wd[...].reshape(rows * 128, 128),
            preferred_element_type=F32,
        )
        for dx in (-1, 0, 1):
            halves = []
            for g in range(fgroups):
                shift = (2 * rows * (g - dx - 1)) % 128
                half = value[8 * g : 8 * g + 8]
                halves.append(pltpu.roll(half, shift, 1) if shift else half)
            cpack[t, dx + 1] = jnp.where(lane8 < 2 * rows, halves[0], halves[1])
            for side, flag, dz in ((0, right, 1), (1, left, -1)):
                remote(
                    ("cp", t, 1 - dx, side),
                    both(in_x[dx], flag),
                    cpack.at[t, dx + 1],
                    cp.at[t, 1 - dx, side],
                    over(dx, dz),
                )

    column_inner(0)
    column_outer(0)
    for t in range(NSUB):
        final = t == NSUB - 1
        col, at_col = (last, ()) if final else (pad, (t + 1,))

        def col_at(r):
            return (*at_col, r + (0 if final else 1))

        box, mine, exported = exs[t], ess[t], []
        for p in range(pairs):
            pair = [ppre[2 * p, 0:flux], ppre[2 * p + 1, 0:flux]]
            if t > 0:
                halves = []
                for r in (2 * p, 2 * p + 1):
                    smooth = stencil(lambda i: dpad[t - 1, i], dedges, fgroups, r)
                    halves.append(jnp.concatenate(split3(smooth, 0), axis=0))
                halves = jnp.concatenate(halves, axis=1)
                dsplit[p] = halves
                product = jnp.dot(acat16[0:flux, : 3 * flux], halves, preferred_element_type=F32)
                pair = [pair[0] + product[:, :128], pair[1] + product[:, 128:]]
            for i, r in enumerate((2 * p, 2 * p + 1)):
                exported.append((jnp.tanh(scales * pair[i]) * wet[r : r + 1, :]).astype(BF16))
                mine[r] = exported[r]
                col[(*col_at(r), slice(0, flux))] = pair[i]
        block = mine.at[0:rows]

        def send_exports():
            remote(("ex", t, 0), nxt, block, box.at[0:rows], over(1, 0))
            remote(("ex", t, 2), prev, block, box.at[2 * rows : 3 * rows], over(-1, 0))
            remote(("ex", t, 1), None, block, box.at[rows : 2 * rows], over(0, 0))

        send_exports()
        if 0 < t < NSUB - 1:
            send_parts(t, exported)
        if not final:
            if t == 0:
                receive("eo0", prev, eff_over.at[0])
                receive("eo1", nxt, eff_over.at[1])
            for k in range(depth):
                above, below = eff_over[0, k], eff_over[1, 4 + k]
                rpack[t, 0, k] = mine[jnp.where(above >= 2 * rows, above - 2 * rows, rows)]
                rpack[t, 1, k] = mine[jnp.where(jnp.logical_and(below >= 0, below < rows), below, rows)]
            remote(("rp", t, 1), prev2, rpack.at[t, 0], rp.at[t, 1], over(-2, 0))
            remote(("rp", t, 0), nxt2, rpack.at[t, 1], rp.at[t, 0], over(2, 0))
        if t > 0:
            for p in range(pairs):
                product = jnp.dot(
                    acat16[flux:, : 3 * flux], dsplit[p], preferred_element_type=F32
                )
                for i, r in enumerate((2 * p, 2 * p + 1)):
                    col[(*col_at(r), slice(flux, lev))] = (
                        ppre[r, flux:] + product[:, i * 128 : (i + 1) * 128]
                    )
        else:
            for r in range(rows):
                col[(*col_at(r), slice(flux, lev))] = ppre[r, flux:]

        if not final:
            pack_rows(t + 1)
            send_rows(t + 1)
            pack_edges(t + 1)
            send_columns(t + 1)
            if t == 0:
                spread_columns()
                send_parts(0, [mine[i] for i in range(rows)])
            column_inner(t + 1)

        receive(("ex", t, 1), None, box.at[rows : 2 * rows])
        receive(("ex", t, 0), prev, box.at[0:rows])
        receive(("ex", t, 2), nxt, box.at[2 * rows : 3 * rows])
        for p in range(pairs):
            picks = [[], []]
            for i in range(2):
                for k in range(depth):
                    at = source_of(2 * p + i, k)
                    picks[i].append(box[jnp.where(at >= 0, at, 3 * rows)])
            parts = pair_product(picks, (w[2 * p], w[2 * p + 1]))
            for i, r in enumerate((2 * p, 2 * p + 1)):
                value = gains * wet[r : r + 1, :] * parts[i]
                if final:
                    last[r, 0:flux] += value
                else:
                    dpad[t, r + 1] = value
        if not final:
            if t == 0:
                receive("es0", prev, eff_same.at[0])
                receive("es1", nxt, eff_same.at[1])
                receive("we0", prev, wedge.at[0])
                receive("we1", nxt, wedge.at[1])
                receive("wn0", prev, wetn.at[0])
                receive("wn1", nxt, wetn.at[1])
                receive("wz0", left, wets.at[0])
                receive("wz1", right, wets.at[1])
                wet_up = jnp.where(ocean, wetn[0, 7:8].astype(F32), 1.0)
                wet_down = jnp.where(ocean, wetn[1, 0:1].astype(F32), 1.0)
                beside = jnp.zeros((8, 128), F32)
                for r in range(rows):
                    for side, have in ((0, 127), (1, 0)):
                        at = 2 * r + side
                        cells = jnp.broadcast_to(wets[side, r : r + 1].astype(F32), (8, 128))
                        beside = jnp.where(
                            lane8 == at, pltpu.roll(cells, (at - have) % 128, 1), beside
                        )
                beside = jnp.where(ocean, beside, 1.0)
                gw[...] = jnp.where(
                    lane8 < 2 * rows,
                    beside * gains[0:8],
                    pltpu.roll(beside, 2 * rows, 1) * gains[8:16],
                )
            receive(("rp", t, 0), prev2, rp.at[t, 0])
            receive(("rp", t, 1), nxt2, rp.at[t, 1])
            picks = [[], []]
            for k in range(depth):
                above, below = eff_same[0, 4 + k], eff_same[1, k]
                here = jnp.where(above >= rows, above - rows, 3 * rows)
                picks[0].append(box[here] + rp[t, 0, k])
                here = jnp.where(jnp.logical_and(below >= 0, below < 2 * rows), below + rows, 3 * rows)
                picks[1].append(box[here] + rp[t, 1, k])
            parts = pair_product(picks, (wedge[0], wedge[1]))
            dpad[t, 0] = gains * wet_up * parts[0]
            dpad[t, rows + 1] = gains * wet_down * parts[1]
            for dx in (-1, 0, 1):
                receive(("cp", t, dx + 1, 0), both(in_x[dx], left), cp.at[t, dx + 1, 0])
                receive(("cp", t, dx + 1, 1), both(in_x[dx], right), cp.at[t, dx + 1, 1])
            dedges = gw[...] * jnp.where(
                lane8 % 2 == 1,
                cp[t, 0, 1] + cp[t, 1, 1] + cp[t, 2, 1],
                cp[t, 0, 0] + cp[t, 1, 0] + cp[t, 2, 0],
            )
            column_outer(t + 1)

    for flag, copy in sent:
        when(flag, copy.wait_send)


def on_device(*args):
    fields, export_scale, tile_source = args[0], args[4], args[6]
    _, lev, rows, width = fields.shape
    flux, depth = export_scale.shape[1], tile_source.shape[3]
    dma = pltpu.SemaphoreType.DMA
    any_ = pl.BlockSpec(memory_space=pl.ANY)
    vmem = pltpu.VMEM
    box = vmem((3 * rows + 1, flux, width), BF16)
    mine = vmem((rows + 1, flux, width), BF16)
    result = pl.pallas_call(
        functools.partial(kernel, (lev, rows, flux, depth)),
        out_shape=pltpu.VMEM((rows, lev, width), F32),
        in_specs=[any_] * 9,
        out_specs=pl.BlockSpec(memory_space=pltpu.VMEM),
        scratch_shapes=[
            vmem((NSUB, rows + 2, lev, width), F32),
            vmem((NSUB - 1, rows + 2, flux, width), F32),
            vmem((NSUB, 2, 24, width), F32),
            vmem((NSUB - 1, 3, 2, 8, width), F32),
            vmem((NSUB - 1, 2, depth, flux, width), BF16),
            vmem((rows, lev, width), F32),
            vmem((NSUB, 2, 80, width), BF16),
            vmem((NSUB, 2, 80, width), BF16),
            vmem((NSUB, 24, width), F32),
            vmem((NSUB - 1, 3, 8, width), F32),
            vmem((NSUB - 1, 2, depth, flux, width), BF16),
            vmem((rows // 2, 3 * flux, 2 * width), BF16),
            vmem((rows, depth, width, width), BF16),
            vmem((2, depth, width, width), BF16),
            vmem((144, width), BF16),
            vmem((3, 144, width), BF16),
            vmem((rows, width, width), BF16),
            vmem((rows, width), F32),
            vmem((rows, width), jnp.int32),
            vmem((rows, width), F32),
            vmem((2, 8, width), jnp.int32),
            vmem((2, rows, width), jnp.int32),
            vmem((8, width), F32),
            vmem((lev, lev), F32),
            vmem((lev, 256), BF16),
            vmem((lev, 128), BF16),
            box,
            box,
            box,
            box,
            mine,
            mine,
            mine,
            mine,
            pltpu.SMEM((8,), jnp.int32),
            pltpu.SMEM((2, 8), jnp.int32),
            pltpu.SMEM((2, 8), jnp.int32),
            pltpu.SMEM((1, flux), F32),
            pltpu.SMEM((1, flux), F32),
            pltpu.SMEM((1, depth, 1, rows), jnp.int32),
            pltpu.SMEM((1, 1, rows), jnp.int32),
            dma((24,)),
            dma((80,)),
            dma((80,)),
        ],
        compiler_params=pltpu.CompilerParams(
            collective_id=0, has_side_effects=True, vmem_limit_bytes=56 * 1024 * 1024
        ),
        name="coupled",
    )(*args[:6], jnp.transpose(args[6], (0, 3, 2, 1)), jnp.transpose(args[7], (0, 2, 1)), args[8])
    return jnp.transpose(result, (1, 0, 2))[None]


def solution(mesh):
    in_specs = (
        P("comp", None, "gx", "gz"),
        P("comp", "gx", "gz"),
        P("gx", "gz"),
        P("comp", None, None),
        P("comp", None),
        P("comp", None),
        P("comp", "gx", "gz", None),
        P("comp", "gx", "gz"),
        P("comp", "gx", "gz", None, None, None),
    )
    out_specs = P("comp", None, "gx", "gz")
    return jax.shard_map(
        on_device, mesh=mesh, in_specs=in_specs, out_specs=out_specs, check_vma=False
    )
```

```python
import functools

import jax
import jax.numpy as jnp
from jax import lax
from jax.experimental import pallas as pl
from jax.experimental.pallas import tpu as pltpu
from jax.sharding import PartitionSpec as P

NSUB = 4
MESH = pl.DeviceIdType.MESH
F32 = jnp.float32
BF16 = jnp.bfloat16


def lane_ids(shape):
    return lax.broadcasted_iota(jnp.int32, shape, 1)


def split3(value, pad):
    if pad:
        value = jnp.concatenate([value, jnp.zeros((pad, value.shape[1]), F32)], axis=0)
    high = value.astype(BF16)
    low = (value - high.astype(F32)).astype(BF16)
    return [high, high, low]


def place(group, row):
    return group // 4, 32 * (group % 4) + 2 * row


def kernel(dims, fields, diff, wetm, op, scale_in, gain_in, source_in, count_in, tiles, out, *scratch):
    lev, rows, flux, depth = dims
    last = out
    (pad, dpad, hz, cp, rp, ppre, hx, hxpack, zpack, cpack, rpack, dsplit, w, wedge, wcol, wcols, wd) = scratch[:17]
    (rate, weti, wet, wetn, wets, gw, ops, acat, acat16) = scratch[17:26]
    exs, ess = scratch[26:30], scratch[30:34]
    eff, eff_same, eff_over, scale, gain, source, count, chosen = scratch[34:42]
    local_sem, send_sem, recv_sem = scratch[42:45]
    groups, fgroups = lev // 8, flux // 8
    pairs = rows // 2
    c, gx, gz = lax.axis_index("comp"), lax.axis_index("gx"), lax.axis_index("gz")
    nx, nz = lax.axis_size("gx"), lax.axis_size("gz")
    prev, nxt, left, right = gx > 0, gx < nx - 1, gz > 0, gz < nz - 1
    prev2, nxt2 = gx > 1, gx < nx - 2

    def same(dx, dz):
        return (c, gx + dx, gz + dz)

    def over(dx, dz):
        return (1 - c, gx + dx, gz + dz)

    in_x = {-1: prev, 0: None, 1: nxt}

    def both(a, b):
        return b if a is None else a if b is None else jnp.logical_and(a, b)

    def when(flag, todo):
        if flag is None:
            todo()
        else:
            pl.when(flag)(todo)

    local = iter(range(100))

    def fetch(src, dst):
        copy = pltpu.make_async_copy(src, dst, local_sem.at[next(local)])
        copy.start()
        return copy

    zeros_w = jnp.zeros((depth, 128, 128), BF16)
    zeros_ex = jnp.zeros((rows, flux, 128), BF16)
    no_source = jnp.concatenate([jnp.zeros((128, 128), BF16), jnp.full((16, 128), -1.0, BF16)], axis=0)

    def blank(flag, x_side):
        @pl.when(jnp.logical_not(flag))
        def _():
            hx[:, x_side] = jnp.zeros((NSUB, 80, 128), BF16)
            for ref in exs:
                ref[2 * rows * x_side : 2 * rows * x_side + rows] = zeros_ex
            wedge[x_side] = zeros_w
            wcols[2 * x_side] = no_source
            wetn[x_side] = jnp.zeros((8, 128), jnp.int32)
            cp[:, 2 * x_side] = jnp.zeros((NSUB - 1, 2, 8, 128), F32)
            for k in range(8):
                eff_same[x_side, k] = -1
                eff_over[x_side, k] = -1

    blank(prev, 0)
    blank(nxt, 1)
    for x_side, flag in ((0, prev2), (1, nxt2)):

        @pl.when(jnp.logical_not(flag))
        def _():
            rp[:, x_side] = jnp.zeros((NSUB - 1, depth, flux, 128), BF16)

    for side, flag in ((0, left), (1, right)):

        @pl.when(jnp.logical_not(flag))
        def _():
            hz[:, side] = jnp.zeros((NSUB, 24, 128), F32)
            cp[:, :, side] = jnp.zeros((NSUB - 1, 3, 8, 128), F32)
            wets[side] = jnp.zeros((rows, 128), jnp.int32)

    for ref in exs:
        ref[3 * rows] = jnp.zeros((flux, 128), BF16)
    for ref in ess:
        ref[rows] = jnp.zeros((flux, 128), BF16)

    barrier = pltpu.get_barrier_semaphore()
    peers = [(None, over(0, 0))]
    peers += [(f, over(dx, 0)) for f, dx in ((prev, -1), (nxt, 1))]
    peers += [(f, same(dx, 0)) for f, dx in ((prev, -1), (nxt, 1))]
    peers += [(f, same(0, dz)) for f, dz in ((left, -1), (right, 1))]
    expected = jnp.int32(0)
    for flag, peer in peers:
        when(
            flag,
            lambda peer=peer: pl.semaphore_signal(
                barrier, inc=1, device_id=peer, device_id_type=MESH
            ),
        )
        expected = expected + (1 if flag is None else flag.astype(jnp.int32))

    state_copies = [fetch(fields.at[0, :, r, :], pad.at[0, r + 1]) for r in range(rows)]
    sources = [fetch(source_in, source), fetch(count_in, count)]
    misc = [fetch(op.at[0], ops), fetch(diff.at[0], rate), fetch(wetm, weti)]
    misc += [fetch(scale_in, scale), fetch(gain_in, gain)]
    tile_copy = fetch(tiles.at[0, :, 0], w)

    for copy in state_copies:
        copy.wait()
    lane8 = lane_ids((8, 128))

    def pack_edges(t):
        parts = [None] * 3
        for r in range(rows):
            for g in range(groups):
                slot, at = place(g, r)
                moved = pltpu.roll(pad[t, r + 1, 8 * g : 8 * g + 8, :], at + 1, 1)
                old = parts[slot]
                parts[slot] = moved if old is None else jnp.where(lane8 // 2 == at // 2, moved, old)
        zpack[t] = jnp.concatenate(parts, axis=0)

    def pack_rows(t):
        for i, at in enumerate((rows, 1)):
            hxpack[t, i] = jnp.concatenate([pad[t, at], jnp.zeros((80 - lev, 128), F32)], axis=0).astype(BF16)

    pack_rows(0)
    pack_edges(0)

    pl.semaphore_wait(barrier, expected)

    ids = {}
    sent = []

    def remote(key, flag, src, dst, peer):
        at = ids.setdefault(key, len(ids))
        copy = pltpu.make_async_remote_copy(
            src_ref=src,
            dst_ref=dst,
            send_sem=send_sem.at[at],
            recv_sem=recv_sem.at[at],
            device_id=peer,
            device_id_type=MESH,
        )
        when(flag, copy.start)
        sent.append((flag, copy))

    def receive(key, flag, dst):
        at = ids[key]
        copy = pltpu.make_async_remote_copy(
            src_ref=dst,
            dst_ref=dst,
            send_sem=send_sem.at[at],
            recv_sem=recv_sem.at[at],
            device_id=over(0, 0),
            device_id_type=MESH,
        )
        when(flag, copy.wait_recv)

    def send_rows(t):
        remote(("hx", t, 0), nxt, hxpack.at[t, 0], hx.at[t, 0], same(1, 0))
        remote(("hx", t, 1), prev, hxpack.at[t, 1], hx.at[t, 1], same(-1, 0))

    def send_columns(t):
        remote(("hz", t, 0), right, zpack.at[t], hz.at[t, 0], same(0, 1))
        remote(("hz", t, 1), left, zpack.at[t], hz.at[t, 1], same(0, -1))

    send_rows(0)
    send_columns(0)

    def send_tiles(part):
        first, final_row = tiles.at[0, 0, 0], tiles.at[0, rows - 1, 0]
        remote(("we", 0, part.start), nxt, final_row.at[part], wedge.at[0, part], same(1, 0))
        remote(("we", 1, part.start), prev, first.at[part], wedge.at[1, part], same(-1, 0))

    parts_of_k = (slice(0, depth),)

    for copy in sources:
        copy.wait()

    def source_of(r, k):
        return jnp.where(k < count[0, 0, r], source[0, k, 0, r], -1)

    index = jnp.full((8, 128), -1, jnp.int32)
    for k in range(depth):
        for r in range(rows):
            at = source_of(r, k)
            chosen[depth * r + k] = jnp.where(at >= 0, at, 3 * rows)
            index = jnp.where(lane8 // 2 == k * rows + r, at, index)
    index = index.astype(F32)
    for k in range(8):
        eff[k] = source_of(0 if k < 4 else rows - 1, k % 4) if k % 4 < depth else -1

    tile_copy.wait()
    lane128 = lane_ids((128, 128))
    packed = jnp.zeros((128, 128), BF16)
    for k in range(depth):
        for r in range(rows):
            at = 2 * (k * rows + r)
            packed = jnp.where(lane128 // 2 == at // 2, pltpu.roll(w[r, k], at + 1, 1), packed)
    wcol[0:128] = packed
    wcol[128:144] = jnp.concatenate([index, index], axis=0).astype(BF16)
    for dx in (-1, 0, 1):
        remote(("wc", 1 - dx), in_x[dx], wcol, wcols.at[1 - dx], over(dx, 0))
    remote("es0", nxt, eff, eff_same.at[0], same(1, 0))
    remote("es1", prev, eff, eff_same.at[1], same(-1, 0))
    remote("eo0", nxt, eff, eff_over.at[0], over(1, 0))
    remote("eo1", prev, eff, eff_over.at[1], over(-1, 0))
    remote("wn0", nxt, wetm.at[rows - 8 : rows], wetn.at[0], same(1, 0))
    remote("wn1", prev, wetm.at[0:8], wetn.at[1], same(-1, 0))
    remote("wz0", right, wetm, wets.at[0], same(0, 1))
    remote("wz1", left, wetm, wets.at[1], same(0, -1))

    send_tiles(parts_of_k[0])

    for copy in misc:
        copy.wait()
    ocean = c == 1
    wet[...] = jnp.where(ocean, weti[...].astype(F32), 1.0)
    rate[...] = rate[...] * wet[...]
    matrix = jnp.concatenate([ops[...], jnp.zeros((lev, 128 - lev), F32)], axis=1)
    high = matrix.astype(BF16).astype(F32)
    low = matrix - high
    lane = lane_ids((lev, 128))
    low80 = pltpu.roll(low, 80, 1)
    acat[...] = jnp.concatenate(
        [jnp.where(lane < 80, high, low80), jnp.where(lane < 32, low80, pltpu.roll(high, 32, 1))],
        axis=1,
    ).astype(BF16)
    acat16[...] = jnp.where(
        lane < flux,
        high,
        jnp.where(
            lane < 2 * flux,
            pltpu.roll(low, flux, 1),
            jnp.where(lane < 3 * flux, pltpu.roll(high, 2 * flux, 1), 0.0),
        ),
    ).astype(BF16)
    level = lax.broadcasted_iota(jnp.int32, (flux, 128), 0)
    scales = jnp.zeros((flux, 128), F32)
    gains = jnp.zeros((flux, 128), F32)
    for f in range(flux):
        scales = jnp.where(level == f, scale[0, f], scales)
        gains = jnp.where(level == f, gain[0, f], gains)


    def merged_edges(t):
        odd = lane_ids((24, 128)) % 2 == 1
        return jnp.where(odd, hz[t, 1], hz[t, 0])

    def stencil(load, edges, n_groups, r):
        here = load(r + 1)
        levels = 8 * n_groups
        lane = lane_ids((levels, 128))
        moved = []
        for g in range(n_groups):
            slot, at = place(g, r)
            moved.append(pltpu.roll(edges[8 * slot : 8 * slot + 8], (127 - at) % 128, 1))
        beyond = jnp.concatenate(moved, axis=0)
        before = pltpu.roll(jnp.where(lane == 127, beyond, here), 1, 1)
        after = pltpu.roll(jnp.where(lane == 0, beyond, here), 127, 1)
        beside = load(r + 2) + load(r) + after + before
        return here + rate[r : r + 1, :] * (beside - 4.0 * here)

    def column_of(t, edges, some):
        def row_of(i):
            if i in (0, rows + 1):
                return hx[t, min(i, 1)].astype(F32)[:lev]
            return pad[t, i]

        for p in some:
            halves = []
            for r in (2 * p, 2 * p + 1):
                smooth = stencil(row_of, edges, groups, r)
                halves.append(
                    jnp.concatenate(split3(smooth, 80 - lev) + [jnp.zeros((16, 128), BF16)], axis=0)
                )
            product = jnp.dot(
                acat[...], jnp.concatenate(halves, axis=1), preferred_element_type=F32
            )
            ppre[2 * p] = product[:, :128]
            ppre[2 * p + 1] = product[:, 128:]

    def column_inner(t):
        receive(("hz", t, 0), left, hz.at[t, 0])
        receive(("hz", t, 1), right, hz.at[t, 1])
        column_of(t, merged_edges(t), range(1, pairs - 1))

    def column_outer(t):
        receive(("hx", t, 0), prev, hx.at[t, 0])
        receive(("hx", t, 1), nxt, hx.at[t, 1])
        column_of(t, merged_edges(t), (0, pairs - 1))

    def pair_product(picks, weights):
        product = jnp.dot(
            jnp.concatenate([jnp.concatenate(row, axis=1) for row in picks], axis=0),
            jnp.concatenate([tile.reshape(depth * 128, 128) for tile in weights], axis=1),
            preferred_element_type=F32,
        )
        return product[:flux, :128], product[flux:, 128:]

    def spread_columns():
        group = lane128 // (2 * rows)
        group8 = lane8 // (2 * rows)
        for dx in (-1, 0, 1):
            receive(("wc", dx + 1), in_x[dx], wcols.at[dx + 1])
        tags, columns = [], []
        for k in range(depth):
            tag = jnp.full((8, 128), -1.0, F32)
            column = jnp.zeros((128, 128), BF16)
            for dx in (-1, 0, 1):
                shift = (2 * rows * (dx + 1 - k)) % 128
                moved, own = wcols[dx + 1, 0:128], wcols[dx + 1, 128:144].astype(F32)[0:8]
                if shift:
                    moved, own = pltpu.roll(moved, shift, 1), pltpu.roll(own, shift, 1)
                tag = jnp.where(group8 == dx + 1, own - float(rows * (1 - dx)), tag)
                column = jnp.where(group == dx + 1, moved, column)
            tags.append(tag[0:1])
            columns.append(column)
        for row in range(rows):
            total = None
            for k in range(depth):
                term = columns[k] * jnp.where(tags[k] == float(row), 1.0, 0.0).astype(BF16)
                total = term if total is None else total + term
            wd[row] = total

    def send_parts(t, exported):
        value = jnp.dot(
            jnp.concatenate(exported, axis=1),
            wd[...].reshape(rows * 128, 128),
            preferred_element_type=F32,
        )
        for dx in (-1, 0, 1):
            halves = []
            for g in range(fgroups):
                shift = (2 * rows * (g - dx - 1)) % 128
                half = value[8 * g : 8 * g + 8]
                halves.append(pltpu.roll(half, shift, 1) if shift else half)
            cpack[t, dx + 1] = jnp.where(lane8 < 2 * rows, halves[0], halves[1])
            for side, flag, dz in ((0, right, 1), (1, left, -1)):
                remote(
                    ("cp", t, 1 - dx, side),
                    both(in_x[dx], flag),
                    cpack.at[t, dx + 1],
                    cp.at[t, 1 - dx, side],
                    over(dx, dz),
                )

    column_inner(0)
    column_outer(0)
    for t in range(NSUB):
        final = t == NSUB - 1
        col, at_col = (last, ()) if final else (pad, (t + 1,))

        def col_at(r):
            return (*at_col, r + (0 if final else 1))

        box, mine, exported = exs[t], ess[t], []
        for p in range(pairs):
            pair = [ppre[2 * p, 0:flux], ppre[2 * p + 1, 0:flux]]
            if t > 0:
                halves = []
                for r in (2 * p, 2 * p + 1):
                    smooth = stencil(lambda i: dpad[t - 1, i], dedges, fgroups, r)
                    halves.append(jnp.concatenate(split3(smooth, 0), axis=0))
                halves = jnp.concatenate(halves, axis=1)
                dsplit[p] = halves
                product = jnp.dot(acat16[0:flux, : 3 * flux], halves, preferred_element_type=F32)
                pair = [pair[0] + product[:, :128], pair[1] + product[:, 128:]]
            for i, r in enumerate((2 * p, 2 * p + 1)):
                exported.append((jnp.tanh(scales * pair[i]) * wet[r : r + 1, :]).astype(BF16))
                mine[r] = exported[r]
                col[(*col_at(r), slice(0, flux))] = pair[i]
        block = mine.at[0:rows]

        def send_exports():
            remote(("ex", t, 0), nxt, block, box.at[0:rows], over(1, 0))
            remote(("ex", t, 2), prev, block, box.at[2 * rows : 3 * rows], over(-1, 0))
            remote(("ex", t, 1), None, block, box.at[rows : 2 * rows], over(0, 0))

        send_exports()
        if 0 < t < NSUB - 1:
            send_parts(t, exported)
        if not final:
            if t == 0:
                receive("eo0", prev, eff_over.at[0])
                receive("eo1", nxt, eff_over.at[1])
            for k in range(depth):
                above, below = eff_over[0, k], eff_over[1, 4 + k]
                rpack[t, 0, k] = mine[jnp.where(above >= 2 * rows, above - 2 * rows, rows)]
                rpack[t, 1, k] = mine[jnp.where(jnp.logical_and(below >= 0, below < rows), below, rows)]
            remote(("rp", t, 1), prev2, rpack.at[t, 0], rp.at[t, 1], over(-2, 0))
            remote(("rp", t, 0), nxt2, rpack.at[t, 1], rp.at[t, 0], over(2, 0))
        if t > 0:
            for p in range(pairs):
                product = jnp.dot(
                    acat16[flux:, : 3 * flux], dsplit[p], preferred_element_type=F32
                )
                for i, r in enumerate((2 * p, 2 * p + 1)):
                    col[(*col_at(r), slice(flux, lev))] = (
                        ppre[r, flux:] + product[:, i * 128 : (i + 1) * 128]
                    )
        else:
            for r in range(rows):
                col[(*col_at(r), slice(flux, lev))] = ppre[r, flux:]

        if not final:
            pack_rows(t + 1)
            send_rows(t + 1)
            pack_edges(t + 1)
            send_columns(t + 1)
            if t == 0:
                spread_columns()
                send_parts(0, [mine[i] for i in range(rows)])
            column_inner(t + 1)

        if final:
            for flag, copy in sent[:-3]:
                when(flag, copy.wait_send)
        receive(("ex", t, 1), None, box.at[rows : 2 * rows])
        receive(("ex", t, 0), prev, box.at[0:rows])
        receive(("ex", t, 2), nxt, box.at[2 * rows : 3 * rows])
        for p in range(pairs):
            picks = [[], []]
            for i in range(2):
                for k in range(depth):
                    picks[i].append(box[chosen[depth * (2 * p + i) + k]])
            parts = pair_product(picks, (w[2 * p], w[2 * p + 1]))
            for i, r in enumerate((2 * p, 2 * p + 1)):
                value = gains * wet[r : r + 1, :] * parts[i]
                if final:
                    last[r, 0:flux] += value
                else:
                    dpad[t, r + 1] = value
        if not final:
            if t == 0:
                receive("es0", prev, eff_same.at[0])
                receive("es1", nxt, eff_same.at[1])
                for part in parts_of_k:
                    receive(("we", 0, part.start), prev, wedge.at[0, part])
                    receive(("we", 1, part.start), nxt, wedge.at[1, part])
                receive("wn0", prev, wetn.at[0])
                receive("wn1", nxt, wetn.at[1])
                receive("wz0", left, wets.at[0])
                receive("wz1", right, wets.at[1])
                wet_up = jnp.where(ocean, wetn[0, 7:8].astype(F32), 1.0)
                wet_down = jnp.where(ocean, wetn[1, 0:1].astype(F32), 1.0)
                beside = jnp.zeros((8, 128), F32)
                for r in range(rows):
                    for side, have in ((0, 127), (1, 0)):
                        at = 2 * r + side
                        cells = jnp.broadcast_to(wets[side, r : r + 1].astype(F32), (8, 128))
                        beside = jnp.where(
                            lane8 == at, pltpu.roll(cells, (at - have) % 128, 1), beside
                        )
                beside = jnp.where(ocean, beside, 1.0)
                gw[...] = jnp.where(
                    lane8 < 2 * rows,
                    beside * gains[0:8],
                    pltpu.roll(beside, 2 * rows, 1) * gains[8:16],
                )
            receive(("rp", t, 0), prev2, rp.at[t, 0])
            receive(("rp", t, 1), nxt2, rp.at[t, 1])
            picks = [[], []]
            for k in range(depth):
                above, below = eff_same[0, 4 + k], eff_same[1, k]
                here = jnp.where(above >= rows, above - rows, 3 * rows)
                picks[0].append(box[here] + rp[t, 0, k])
                here = jnp.where(jnp.logical_and(below >= 0, below < 2 * rows), below + rows, 3 * rows)
                picks[1].append(box[here] + rp[t, 1, k])
            parts = pair_product(picks, (wedge[0], wedge[1]))
            dpad[t, 0] = gains * wet_up * parts[0]
            dpad[t, rows + 1] = gains * wet_down * parts[1]
            for dx in (-1, 0, 1):
                receive(("cp", t, dx + 1, 0), both(in_x[dx], left), cp.at[t, dx + 1, 0])
                receive(("cp", t, dx + 1, 1), both(in_x[dx], right), cp.at[t, dx + 1, 1])
            dedges = gw[...] * jnp.where(
                lane8 % 2 == 1,
                cp[t, 0, 1] + cp[t, 1, 1] + cp[t, 2, 1],
                cp[t, 0, 0] + cp[t, 1, 0] + cp[t, 2, 0],
            )
            column_outer(t + 1)

    for flag, copy in sent[-3:]:
        when(flag, copy.wait_send)


def on_device(*args):
    fields, export_scale, tile_source = args[0], args[4], args[6]
    _, lev, rows, width = fields.shape
    flux, depth = export_scale.shape[1], tile_source.shape[3]
    dma = pltpu.SemaphoreType.DMA
    any_ = pl.BlockSpec(memory_space=pl.ANY)
    vmem = pltpu.VMEM
    box = vmem((3 * rows + 1, flux, width), BF16)
    mine = vmem((rows + 1, flux, width), BF16)
    result = pl.pallas_call(
        functools.partial(kernel, (lev, rows, flux, depth)),
        out_shape=pltpu.VMEM((rows, lev, width), F32),
        in_specs=[any_] * 9,
        out_specs=pl.BlockSpec(memory_space=pltpu.VMEM),
        scratch_shapes=[
            vmem((NSUB, rows + 2, lev, width), F32),
            vmem((NSUB - 1, rows + 2, flux, width), F32),
            vmem((NSUB, 2, 24, width), F32),
            vmem((NSUB - 1, 3, 2, 8, width), F32),
            vmem((NSUB - 1, 2, depth, flux, width), BF16),
            vmem((rows, lev, width), F32),
            vmem((NSUB, 2, 80, width), BF16),
            vmem((NSUB, 2, 80, width), BF16),
            vmem((NSUB, 24, width), F32),
            vmem((NSUB - 1, 3, 8, width), F32),
            vmem((NSUB - 1, 2, depth, flux, width), BF16),
            vmem((rows // 2, 3 * flux, 2 * width), BF16),
            vmem((rows, depth, width, width), BF16),
            vmem((2, depth, width, width), BF16),
            vmem((144, width), BF16),
            vmem((3, 144, width), BF16),
            vmem((rows, width, width), BF16),
            vmem((rows, width), F32),
            vmem((rows, width), jnp.int32),
            vmem((rows, width), F32),
            vmem((2, 8, width), jnp.int32),
            vmem((2, rows, width), jnp.int32),
            vmem((8, width), F32),
            vmem((lev, lev), F32),
            vmem((lev, 256), BF16),
            vmem((lev, 128), BF16),
            box,
            box,
            box,
            box,
            mine,
            mine,
            mine,
            mine,
            pltpu.SMEM((8,), jnp.int32),
            pltpu.SMEM((2, 8), jnp.int32),
            pltpu.SMEM((2, 8), jnp.int32),
            pltpu.SMEM((1, flux), F32),
            pltpu.SMEM((1, flux), F32),
            pltpu.SMEM((1, depth, 1, rows), jnp.int32),
            pltpu.SMEM((1, 1, rows), jnp.int32),
            pltpu.SMEM((rows * depth,), jnp.int32),
            dma((24,)),
            dma((80,)),
            dma((80,)),
        ],
        compiler_params=pltpu.CompilerParams(
            collective_id=0, has_side_effects=True, vmem_limit_bytes=56 * 1024 * 1024
        ),
        name="coupled",
    )(*args[:6], jnp.transpose(args[6], (0, 3, 2, 1)), jnp.transpose(args[7], (0, 2, 1)), args[8])
    return jnp.transpose(result, (1, 0, 2))[None]


def solution(mesh):
    in_specs = (
        P("comp", None, "gx", "gz"),
        P("comp", "gx", "gz"),
        P("gx", "gz"),
        P("comp", None, None),
        P("comp", None),
        P("comp", None),
        P("comp", "gx", "gz", None),
        P("comp", "gx", "gz"),
        P("comp", "gx", "gz", None, None, None),
    )
    out_specs = P("comp", None, "gx", "gz")
    return jax.shard_map(
        on_device, mesh=mesh, in_specs=in_specs, out_specs=out_specs, check_vma=False
    )
```

```python
import functools

import jax
import jax.numpy as jnp
from jax import lax
from jax.experimental import pallas as pl
from jax.experimental.pallas import tpu as pltpu
from jax.sharding import PartitionSpec as P

NSUB = 4
MESH = pl.DeviceIdType.MESH
F32 = jnp.float32
BF16 = jnp.bfloat16


def lane_ids(shape):
    return lax.broadcasted_iota(jnp.int32, shape, 1)


def split3(value, pad):
    if pad:
        value = jnp.concatenate([value, jnp.zeros((pad, value.shape[1]), F32)], axis=0)
    high = value.astype(BF16)
    low = (value - high.astype(F32)).astype(BF16)
    return [high, high, low]


def place(group, row):
    return group // 4, 32 * (group % 4) + 2 * row


def kernel(dims, fields, diff, wetm, op, scale_in, gain_in, source_in, count_in, tiles, out, *scratch):
    lev, rows, flux, depth = dims
    last = out
    (pad, dpad, hz, cp, rp, ppre, hx, hxpack, zpack, cpack, rpack, dsplit, w, wedge, wcol, wcols, wd) = scratch[:17]
    (rate, weti, wet, wetn, wets, gw, ops, acat, acat16) = scratch[17:26]
    exs, ess = scratch[26:30], scratch[30:34]
    eff, eff_same, eff_over, scale, gain, source, count = scratch[34:41]
    local_sem, send_sem, recv_sem = scratch[41:44]
    groups, fgroups = lev // 8, flux // 8
    pairs = rows // 2
    c, gx, gz = lax.axis_index("comp"), lax.axis_index("gx"), lax.axis_index("gz")
    nx, nz = lax.axis_size("gx"), lax.axis_size("gz")
    prev, nxt, left, right = gx > 0, gx < nx - 1, gz > 0, gz < nz - 1
    prev2, nxt2 = gx > 1, gx < nx - 2

    def same(dx, dz):
        return (c, gx + dx, gz + dz)

    def over(dx, dz):
        return (1 - c, gx + dx, gz + dz)

    in_x = {-1: prev, 0: None, 1: nxt}

    def both(a, b):
        return b if a is None else a if b is None else jnp.logical_and(a, b)

    def when(flag, todo):
        if flag is None:
            todo()
        else:
            pl.when(flag)(todo)

    local = iter(range(100))

    def fetch(src, dst):
        copy = pltpu.make_async_copy(src, dst, local_sem.at[next(local)])
        copy.start()
        return copy

    zeros_w = jnp.zeros((depth, 128, 128), BF16)
    zeros_ex = jnp.zeros((rows, flux, 128), BF16)
    no_source = jnp.concatenate([jnp.zeros((128, 128), BF16), jnp.full((16, 128), -1.0, BF16)], axis=0)

    def blank(flag, x_side):
        @pl.when(jnp.logical_not(flag))
        def _():
            hx[:, x_side] = jnp.zeros((NSUB, 80, 128), BF16)
            for ref in exs:
                ref[2 * rows * x_side : 2 * rows * x_side + rows] = zeros_ex
            wedge[x_side] = zeros_w
            wcols[2 * x_side] = no_source
            wetn[x_side] = jnp.zeros((8, 128), jnp.int32)
            cp[:, 2 * x_side] = jnp.zeros((NSUB - 1, 2, 8, 128), F32)
            for k in range(8):
                eff_same[x_side, k] = -1
                eff_over[x_side, k] = -1

    blank(prev, 0)
    blank(nxt, 1)
    for x_side, flag in ((0, prev2), (1, nxt2)):

        @pl.when(jnp.logical_not(flag))
        def _():
            rp[:, x_side] = jnp.zeros((NSUB - 1, depth, flux, 128), BF16)

    for side, flag in ((0, left), (1, right)):

        @pl.when(jnp.logical_not(flag))
        def _():
            hz[:, side] = jnp.zeros((NSUB, 24, 128), F32)
            cp[:, :, side] = jnp.zeros((NSUB - 1, 3, 8, 128), F32)
            wets[side] = jnp.zeros((rows, 128), jnp.int32)

    for ref in exs:
        ref[3 * rows] = jnp.zeros((flux, 128), BF16)
    for ref in ess:
        ref[rows] = jnp.zeros((flux, 128), BF16)

    barrier = pltpu.get_barrier_semaphore()
    peers = [(None, over(0, 0))]
    peers += [(f, over(dx, 0)) for f, dx in ((prev, -1), (nxt, 1))]
    peers += [(f, same(dx, 0)) for f, dx in ((prev, -1), (nxt, 1))]
    peers += [(f, same(0, dz)) for f, dz in ((left, -1), (right, 1))]
    expected = jnp.int32(0)
    for flag, peer in peers:
        when(
            flag,
            lambda peer=peer: pl.semaphore_signal(
                barrier, inc=1, device_id=peer, device_id_type=MESH
            ),
        )
        expected = expected + (1 if flag is None else flag.astype(jnp.int32))

    misc = [fetch(op.at[0], ops), fetch(diff.at[0], rate), fetch(wetm, weti)]
    misc += [fetch(scale_in, scale), fetch(gain_in, gain), fetch(source_in, source), fetch(count_in, count)]
    state_copies = [fetch(fields.at[0, :, r, :], pad.at[0, r + 1]) for r in range(rows)]
    tile_copy = fetch(tiles.at[0, :, 0], w)

    for copy in misc:
        copy.wait()
    ocean = c == 1
    wet[...] = jnp.where(ocean, weti[...].astype(F32), 1.0)
    rate[...] = rate[...] * wet[...]
    matrix = jnp.concatenate([ops[...], jnp.zeros((lev, 128 - lev), F32)], axis=1)
    high = matrix.astype(BF16).astype(F32)
    low = matrix - high
    lane = lane_ids((lev, 128))
    low80 = pltpu.roll(low, 80, 1)
    acat[...] = jnp.concatenate(
        [jnp.where(lane < 80, high, low80), jnp.where(lane < 32, low80, pltpu.roll(high, 32, 1))],
        axis=1,
    ).astype(BF16)
    acat16[...] = jnp.where(
        lane < flux,
        high,
        jnp.where(
            lane < 2 * flux,
            pltpu.roll(low, flux, 1),
            jnp.where(lane < 3 * flux, pltpu.roll(high, 2 * flux, 1), 0.0),
        ),
    ).astype(BF16)
    level = lax.broadcasted_iota(jnp.int32, (flux, 128), 0)
    scales = jnp.zeros((flux, 128), F32)
    gains = jnp.zeros((flux, 128), F32)
    for f in range(flux):
        scales = jnp.where(level == f, scale[0, f], scales)
        gains = jnp.where(level == f, gain[0, f], gains)

    def source_of(r, k):
        return jnp.where(k < count[0, 0, r], source[0, k, 0, r], -1)

    lane8 = lane_ids((8, 128))
    index = jnp.full((8, 128), -1, jnp.int32)
    for k in range(depth):
        for r in range(rows):
            index = jnp.where(lane8 // 2 == k * rows + r, source_of(r, k), index)
    index = index.astype(F32)
    for k in range(8):
        eff[k] = source_of(0 if k < 4 else rows - 1, k % 4) if k % 4 < depth else -1

    for copy in state_copies:
        copy.wait()

    def pack_edges(t):
        parts = [None] * 3
        for r in range(rows):
            for g in range(groups):
                slot, at = place(g, r)
                moved = pltpu.roll(pad[t, r + 1, 8 * g : 8 * g + 8, :], at + 1, 1)
                old = parts[slot]
                parts[slot] = moved if old is None else jnp.where(lane8 // 2 == at // 2, moved, old)
        zpack[t] = jnp.concatenate(parts, axis=0)

    def pack_rows(t):
        for i, at in enumerate((rows, 1)):
            hxpack[t, i] = jnp.concatenate([pad[t, at], jnp.zeros((80 - lev, 128), F32)], axis=0).astype(BF16)

    pack_rows(0)
    pack_edges(0)

    pl.semaphore_wait(barrier, expected)

    ids = {}
    sent = []

    def remote(key, flag, src, dst, peer):
        at = ids.setdefault(key, len(ids))
        copy = pltpu.make_async_remote_copy(
            src_ref=src,
            dst_ref=dst,
            send_sem=send_sem.at[at],
            recv_sem=recv_sem.at[at],
            device_id=peer,
            device_id_type=MESH,
        )
        when(flag, copy.start)
        sent.append((flag, copy))

    def receive(key, flag, dst):
        at = ids[key]
        copy = pltpu.make_async_remote_copy(
            src_ref=dst,
            dst_ref=dst,
            send_sem=send_sem.at[at],
            recv_sem=recv_sem.at[at],
            device_id=over(0, 0),
            device_id_type=MESH,
        )
        when(flag, copy.wait_recv)

    def send_rows(t):
        remote(("hx", t, 0), nxt, hxpack.at[t, 0], hx.at[t, 0], same(1, 0))
        remote(("hx", t, 1), prev, hxpack.at[t, 1], hx.at[t, 1], same(-1, 0))

    def send_columns(t):
        remote(("hz", t, 0), right, zpack.at[t], hz.at[t, 0], same(0, 1))
        remote(("hz", t, 1), left, zpack.at[t], hz.at[t, 1], same(0, -1))

    send_rows(0)
    send_columns(0)
    first, final_row = tiles.at[0, 0, 0], tiles.at[0, rows - 1, 0]
    remote("es0", nxt, eff, eff_same.at[0], same(1, 0))
    remote("es1", prev, eff, eff_same.at[1], same(-1, 0))
    remote("eo0", nxt, eff, eff_over.at[0], over(1, 0))
    remote("eo1", prev, eff, eff_over.at[1], over(-1, 0))
    remote("wn0", nxt, wetm.at[rows - 8 : rows], wetn.at[0], same(1, 0))
    remote("wn1", prev, wetm.at[0:8], wetn.at[1], same(-1, 0))
    remote("wz0", right, wetm, wets.at[0], same(0, 1))
    remote("wz1", left, wetm, wets.at[1], same(0, -1))

    tile_copy.wait()
    lane128 = lane_ids((128, 128))
    packed = jnp.zeros((128, 128), BF16)
    for k in range(depth):
        for r in range(rows):
            at = 2 * (k * rows + r)
            packed = jnp.where(lane128 // 2 == at // 2, pltpu.roll(w[r, k], at + 1, 1), packed)
    wcol[0:128] = packed
    wcol[128:144] = jnp.concatenate([index, index], axis=0).astype(BF16)
    for dx in (-1, 0, 1):
        remote(("wc", 1 - dx), in_x[dx], wcol, wcols.at[1 - dx], over(dx, 0))
    remote("we0", nxt, final_row, wedge.at[0], same(1, 0))
    remote("we1", prev, first, wedge.at[1], same(-1, 0))

    def merged_edges(t):
        odd = lane_ids((24, 128)) % 2 == 1
        return jnp.where(odd, hz[t, 1], hz[t, 0])

    def stencil(load, edges, n_groups, r):
        here = load(r + 1)
        levels = 8 * n_groups
        lane = lane_ids((levels, 128))
        moved = []
        for g in range(n_groups):
            slot, at = place(g, r)
            moved.append(pltpu.roll(edges[8 * slot : 8 * slot + 8], (127 - at) % 128, 1))
        beyond = jnp.concatenate(moved, axis=0)
        before = pltpu.roll(jnp.where(lane == 127, beyond, here), 1, 1)
        after = pltpu.roll(jnp.where(lane == 0, beyond, here), 127, 1)
        beside = load(r + 2) + load(r) + after + before
        return here + rate[r : r + 1, :] * (beside - 4.0 * here)

    def column_of(t, edges, some):
        def row_of(i):
            if i in (0, rows + 1):
                return hx[t, min(i, 1)].astype(F32)[:lev]
            return pad[t, i]

        for p in some:
            halves = []
            for r in (2 * p, 2 * p + 1):
                smooth = stencil(row_of, edges, groups, r)
                halves.append(
                    jnp.concatenate(split3(smooth, 80 - lev) + [jnp.zeros((16, 128), BF16)], axis=0)
                )
            product = jnp.dot(
                acat[...], jnp.concatenate(halves, axis=1), preferred_element_type=F32
            )
            ppre[2 * p] = product[:, :128]
            ppre[2 * p + 1] = product[:, 128:]

    def column_inner(t):
        receive(("hz", t, 0), left, hz.at[t, 0])
        receive(("hz", t, 1), right, hz.at[t, 1])
        column_of(t, merged_edges(t), range(1, pairs - 1))

    def column_outer(t):
        receive(("hx", t, 0), prev, hx.at[t, 0])
        receive(("hx", t, 1), nxt, hx.at[t, 1])
        column_of(t, merged_edges(t), (0, pairs - 1))

    def pair_product(picks, weights):
        product = jnp.dot(
            jnp.concatenate([jnp.concatenate(row, axis=1) for row in picks], axis=0),
            jnp.concatenate([tile.reshape(depth * 128, 128) for tile in weights], axis=1),
            preferred_element_type=F32,
        )
        return product[:flux, :128], product[flux:, 128:]

    def spread_columns():
        group = lane128 // (2 * rows)
        group8 = lane8 // (2 * rows)
        for dx in (-1, 0, 1):
            receive(("wc", dx + 1), in_x[dx], wcols.at[dx + 1])
        tags, columns = [], []
        for k in range(depth):
            tag = jnp.full((8, 128), -1.0, F32)
            column = jnp.zeros((128, 128), BF16)
            for dx in (-1, 0, 1):
                shift = (2 * rows * (dx + 1 - k)) % 128
                moved, own = wcols[dx + 1, 0:128], wcols[dx + 1, 128:144].astype(F32)[0:8]
                if shift:
                    moved, own = pltpu.roll(moved, shift, 1), pltpu.roll(own, shift, 1)
                tag = jnp.where(group8 == dx + 1, own - float(rows * (1 - dx)), tag)
                column = jnp.where(group == dx + 1, moved, column)
            tags.append(tag[0:1])
            columns.append(column)
        for row in range(rows):
            total = None
            for k in range(depth):
                term = columns[k] * jnp.where(tags[k] == float(row), 1.0, 0.0).astype(BF16)
                total = term if total is None else total + term
            wd[row] = total

    def send_parts(t, exported):
        value = jnp.dot(
            jnp.concatenate(exported, axis=1),
            wd[...].reshape(rows * 128, 128),
            preferred_element_type=F32,
        )
        for dx in (-1, 0, 1):
            halves = []
            for g in range(fgroups):
                shift = (2 * rows * (g - dx - 1)) % 128
                half = value[8 * g : 8 * g + 8]
                halves.append(pltpu.roll(half, shift, 1) if shift else half)
            cpack[t, dx + 1] = jnp.where(lane8 < 2 * rows, halves[0], halves[1])
            for side, flag, dz in ((0, right, 1), (1, left, -1)):
                remote(
                    ("cp", t, 1 - dx, side),
                    both(in_x[dx], flag),
                    cpack.at[t, dx + 1],
                    cp.at[t, 1 - dx, side],
                    over(dx, dz),
                )

    column_inner(0)
    column_outer(0)
    for t in range(NSUB):
        final = t == NSUB - 1
        col, at_col = (last, ()) if final else (pad, (t + 1,))

        def col_at(r):
            return (*at_col, r + (0 if final else 1))

        box, mine, exported = exs[t], ess[t], []
        for p in range(pairs):
            pair = [ppre[2 * p, 0:flux], ppre[2 * p + 1, 0:flux]]
            if t > 0:
                halves = []
                for r in (2 * p, 2 * p + 1):
                    smooth = stencil(lambda i: dpad[t - 1, i], dedges, fgroups, r)
                    halves.append(jnp.concatenate(split3(smooth, 0), axis=0))
                halves = jnp.concatenate(halves, axis=1)
                dsplit[p] = halves
                product = jnp.dot(acat16[0:flux, : 3 * flux], halves, preferred_element_type=F32)
                pair = [pair[0] + product[:, :128], pair[1] + product[:, 128:]]
            for i, r in enumerate((2 * p, 2 * p + 1)):
                exported.append((jnp.tanh(scales * pair[i]) * wet[r : r + 1, :]).astype(BF16))
                mine[r] = exported[r]
                col[(*col_at(r), slice(0, flux))] = pair[i]
            if p == pairs // 2 - 1:
                half = rows // 2
                for i, flag, dx in ((0, nxt, 1), (2, prev, -1)):
                    at = i * rows
                    remote(("eh", t, i, 0), flag, mine.at[0 * half : (0 + 1) * half], box.at[at + 0 * half : at + (0 + 1) * half], over(dx, 0))
        block = mine.at[0:rows]

        def send_exports():
            remote(("ex", t, 0), nxt, block, box.at[0:rows], over(1, 0))
            remote(("ex", t, 2), prev, block, box.at[2 * rows : 3 * rows], over(-1, 0))
            remote(("ex", t, 1), None, block, box.at[rows : 2 * rows], over(0, 0))

        half = rows // 2
        for i, flag, dx in ((0, nxt, 1), (2, prev, -1)):
            at = i * rows
            remote(("eh", t, i, 1), flag, mine.at[1 * half : (1 + 1) * half], box.at[at + 1 * half : at + (1 + 1) * half], over(dx, 0))
        remote(("ex", t, 1), None, mine.at[0:rows], box.at[rows : 2 * rows], over(0, 0))
        if 0 < t < NSUB - 1:
            send_parts(t, exported)
        if not final:
            if t == 0:
                receive("eo0", prev, eff_over.at[0])
                receive("eo1", nxt, eff_over.at[1])
            for k in range(depth):
                above, below = eff_over[0, k], eff_over[1, 4 + k]
                rpack[t, 0, k] = mine[jnp.where(above >= 2 * rows, above - 2 * rows, rows)]
                rpack[t, 1, k] = mine[jnp.where(jnp.logical_and(below >= 0, below < rows), below, rows)]
            remote(("rp", t, 1), prev2, rpack.at[t, 0], rp.at[t, 1], over(-2, 0))
            remote(("rp", t, 0), nxt2, rpack.at[t, 1], rp.at[t, 0], over(2, 0))
        if t > 0:
            for p in range(pairs):
                product = jnp.dot(
                    acat16[flux:, : 3 * flux], dsplit[p], preferred_element_type=F32
                )
                for i, r in enumerate((2 * p, 2 * p + 1)):
                    col[(*col_at(r), slice(flux, lev))] = (
                        ppre[r, flux:] + product[:, i * 128 : (i + 1) * 128]
                    )
        else:
            for r in range(rows):
                col[(*col_at(r), slice(flux, lev))] = ppre[r, flux:]

        if not final:
            pack_rows(t + 1)
            send_rows(t + 1)
            pack_edges(t + 1)
            send_columns(t + 1)
            if t == 0:
                spread_columns()
                send_parts(0, [mine[i] for i in range(rows)])
            column_inner(t + 1)

        receive(("ex", t, 1), None, box.at[rows : 2 * rows])
        for h in range(2):
            receive(("eh", t, 0, h), prev, box.at[h * half : (h + 1) * half])
            receive(("eh", t, 2, h), nxt, box.at[2 * rows + h * half : 2 * rows + (h + 1) * half])
        for p in range(pairs):
            picks = [[], []]
            for i in range(2):
                for k in range(depth):
                    at = source_of(2 * p + i, k)
                    picks[i].append(box[jnp.where(at >= 0, at, 3 * rows)])
            parts = pair_product(picks, (w[2 * p], w[2 * p + 1]))
            for i, r in enumerate((2 * p, 2 * p + 1)):
                value = gains * wet[r : r + 1, :] * parts[i]
                if final:
                    last[r, 0:flux] += value
                else:
                    dpad[t, r + 1] = value
        if not final:
            if t == 0:
                receive("es0", prev, eff_same.at[0])
                receive("es1", nxt, eff_same.at[1])
                receive("we0", prev, wedge.at[0])
                receive("we1", nxt, wedge.at[1])
                receive("wn0", prev, wetn.at[0])
                receive("wn1", nxt, wetn.at[1])
                receive("wz0", left, wets.at[0])
                receive("wz1", right, wets.at[1])
                wet_up = jnp.where(ocean, wetn[0, 7:8].astype(F32), 1.0)
                wet_down = jnp.where(ocean, wetn[1, 0:1].astype(F32), 1.0)
                beside = jnp.zeros((8, 128), F32)
                for r in range(rows):
                    for side, have in ((0, 127), (1, 0)):
                        at = 2 * r + side
                        cells = jnp.broadcast_to(wets[side, r : r + 1].astype(F32), (8, 128))
                        beside = jnp.where(
                            lane8 == at, pltpu.roll(cells, (at - have) % 128, 1), beside
                        )
                beside = jnp.where(ocean, beside, 1.0)
                gw[...] = jnp.where(
                    lane8 < 2 * rows,
                    beside * gains[0:8],
                    pltpu.roll(beside, 2 * rows, 1) * gains[8:16],
                )
            receive(("rp", t, 0), prev2, rp.at[t, 0])
            receive(("rp", t, 1), nxt2, rp.at[t, 1])
            picks = [[], []]
            for k in range(depth):
                above, below = eff_same[0, 4 + k], eff_same[1, k]
                here = jnp.where(above >= rows, above - rows, 3 * rows)
                picks[0].append(box[here] + rp[t, 0, k])
                here = jnp.where(jnp.logical_and(below >= 0, below < 2 * rows), below + rows, 3 * rows)
                picks[1].append(box[here] + rp[t, 1, k])
            parts = pair_product(picks, (wedge[0], wedge[1]))
            dpad[t, 0] = gains * wet_up * parts[0]
            dpad[t, rows + 1] = gains * wet_down * parts[1]
            for dx in (-1, 0, 1):
                receive(("cp", t, dx + 1, 0), both(in_x[dx], left), cp.at[t, dx + 1, 0])
                receive(("cp", t, dx + 1, 1), both(in_x[dx], right), cp.at[t, dx + 1, 1])
            dedges = gw[...] * jnp.where(
                lane8 % 2 == 1,
                cp[t, 0, 1] + cp[t, 1, 1] + cp[t, 2, 1],
                cp[t, 0, 0] + cp[t, 1, 0] + cp[t, 2, 0],
            )
            column_outer(t + 1)

    for flag, copy in sent:
        when(flag, copy.wait_send)


def on_device(*args):
    fields, export_scale, tile_source = args[0], args[4], args[6]
    _, lev, rows, width = fields.shape
    flux, depth = export_scale.shape[1], tile_source.shape[3]
    dma = pltpu.SemaphoreType.DMA
    any_ = pl.BlockSpec(memory_space=pl.ANY)
    vmem = pltpu.VMEM
    box = vmem((3 * rows + 1, flux, width), BF16)
    mine = vmem((rows + 1, flux, width), BF16)
    result = pl.pallas_call(
        functools.partial(kernel, (lev, rows, flux, depth)),
        out_shape=pltpu.VMEM((rows, lev, width), F32),
        in_specs=[any_] * 9,
        out_specs=pl.BlockSpec(memory_space=pltpu.VMEM),
        scratch_shapes=[
            vmem((NSUB, rows + 2, lev, width), F32),
            vmem((NSUB - 1, rows + 2, flux, width), F32),
            vmem((NSUB, 2, 24, width), F32),
            vmem((NSUB - 1, 3, 2, 8, width), F32),
            vmem((NSUB - 1, 2, depth, flux, width), BF16),
            vmem((rows, lev, width), F32),
            vmem((NSUB, 2, 80, width), BF16),
            vmem((NSUB, 2, 80, width), BF16),
            vmem((NSUB, 24, width), F32),
            vmem((NSUB - 1, 3, 8, width), F32),
            vmem((NSUB - 1, 2, depth, flux, width), BF16),
            vmem((rows // 2, 3 * flux, 2 * width), BF16),
            vmem((rows, depth, width, width), BF16),
            vmem((2, depth, width, width), BF16),
            vmem((144, width), BF16),
            vmem((3, 144, width), BF16),
            vmem((rows, width, width), BF16),
            vmem((rows, width), F32),
            vmem((rows, width), jnp.int32),
            vmem((rows, width), F32),
            vmem((2, 8, width), jnp.int32),
            vmem((2, rows, width), jnp.int32),
            vmem((8, width), F32),
            vmem((lev, lev), F32),
            vmem((lev, 256), BF16),
            vmem((lev, 128), BF16),
            box,
            box,
            box,
            box,
            mine,
            mine,
            mine,
            mine,
            pltpu.SMEM((8,), jnp.int32),
            pltpu.SMEM((2, 8), jnp.int32),
            pltpu.SMEM((2, 8), jnp.int32),
            pltpu.SMEM((1, flux), F32),
            pltpu.SMEM((1, flux), F32),
            pltpu.SMEM((1, depth, 1, rows), jnp.int32),
            pltpu.SMEM((1, 1, rows), jnp.int32),
            dma((24,)),
            dma((80,)),
            dma((80,)),
        ],
        compiler_params=pltpu.CompilerParams(
            collective_id=0, has_side_effects=True, vmem_limit_bytes=56 * 1024 * 1024
        ),
        name="coupled",
    )(*args[:6], jnp.transpose(args[6], (0, 3, 2, 1)), jnp.transpose(args[7], (0, 2, 1)), args[8])
    return jnp.transpose(result, (1, 0, 2))[None]


def solution(mesh):
    in_specs = (
        P("comp", None, "gx", "gz"),
        P("comp", "gx", "gz"),
        P("gx", "gz"),
        P("comp", None, None),
        P("comp", None),
        P("comp", None),
        P("comp", "gx", "gz", None),
        P("comp", "gx", "gz"),
        P("comp", "gx", "gz", None, None, None),
    )
    out_specs = P("comp", None, "gx", "gz")
    return jax.shard_map(
        on_device, mesh=mesh, in_specs=in_specs, out_specs=out_specs, check_vma=False
    )
```
